512 devices in a mesh: dp: 8 (over y_hi, core), domain: 64 (over y_lo, x, z).
Axes of the slice: x: 4, y: 8 (y_hi: 4, y_lo: 2; y = y_hi * 2 + y_lo), z: 8, core: 2. Of those that a mesh axis runs over, the one named last changes fastest.
Arguments:
- inputs: bfloat16 [8, 192, 64, 2304], P('dp', 'domain'), may hold values from -6 to 6
- preact: bfloat16 [8, 192, 64, 2304], P('dp', 'domain'), may hold values from -4 to 4
- spectral_weight: bfloat16 [128, 256, 64, 128], P('dp', 'domain'), may hold values from -6 to 6
- point_weight: bfloat16 [64, 64], replicated, may hold values from -0.75 to 0.75
- readout: float32 [48, 2, 64], replicated, may hold values from -0.75 to 0.75
- observed: float32 [8, 2, 32768], P('dp', None, 'domain'), may hold values from -4 to 4
- cell_index: int32 [8, 32768], P('dp', 'domain'), may hold values from 0 to 6911
- drift_steps: int32 [8, 32768], P('dp', 'domain'), may hold values from 0 to 47
- counts: int32 [8, 64], P('dp', 'domain'), may hold values from 1 to 512, as said below
Outputs:
- input_grad: bfloat16 [8, 192, 64, 2304], P('dp', 'domain')
- weight_grad: bfloat16 [128, 256, 64, 128], P('dp', 'domain')
The draws below stay inside these ranges and needn't reach their ends.
Inputs may be any that keep to these rules, and one draw needn't show every extreme that they name: `counts`: for every case some slab has exactly 512 live slots; slots at or beyond a slab's count carry no loss. `cell_index`: cell within the slab: row within the slab times 2304 plus longitude.
All inputs are finite; a program needn't handle non-finite values.
Results may differ from the reference program's by a relative error of at most 0.025.
Values may be sent and summed in bfloat16 or wider, within the bound.
No kernel may reach another device: no remote copies, remote signals or barrier semaphores. Data moves between devices by JAX's collectives and lax.ppermute only.
A program may use at most 64 MiB of HBM per device.

```python
import jax
import jax.numpy as jnp
from jax import lax

C = 64
NX = 2304
NY = 2160
KX = 256
KY = 128
STEPS = 48
ROWS_DEV = 3
SLOTS = 512
CASES = 8
ROWS = 192
N_DOMAIN = 64


def draw_counts(key, part):
    key = jax.random.fold_in(key, 11)
    first, second = jax.random.split(key)
    drawn = jax.random.randint(first, (CASES, N_DOMAIN), 1, SLOTS + 1)
    fullest = jax.random.randint(second, (CASES, 1), 0, N_DOMAIN)
    slab_ids = jnp.arange(N_DOMAIN, dtype=jnp.int32)[None, :]
    return jnp.where(slab_ids == fullest, SLOTS, drawn).astype(jnp.int32)


def with_ends(values, rng, low, largest):
    extent = values.shape
    place = [jax.random.randint(jax.random.fold_in(rng, axis), (), 0, extent[axis]) for axis in range(len(extent))]
    values = values.at[tuple(place)].set(low)
    longest = extent.index(max(extent))
    place[longest] = (place[longest] + 1) % extent[longest]
    return values.at[tuple(place)].set(largest)


def shard_levels(rng, dims, pieces, smallest, high):
    factor_of = 1.0
    for position, blocks in pieces:
        heights = jax.random.uniform(jax.random.fold_in(jax.random.fold_in(rng, 6), position), (blocks,), jnp.float32, smallest / len(pieces), high / len(pieces))
        factor_of = factor_of * jnp.repeat(jnp.exp(heights), dims[position] // blocks).reshape((-1,) + (1,) * (len(dims) - 1 - position))
    return factor_of


def bell_draw(own_key, dims, deviation, bound, cuts=(), kind=jnp.bfloat16):
    array = deviation * jax.random.normal(own_key, dims, jnp.float32)
    if cuts:
        array = array * shard_levels(own_key, dims, cuts, -0.22, 0.18)
    return jnp.clip(array, -bound, bound).astype(kind)


def setup_inputs(seed: int = 0) -> dict:
    key_of = jax.random.split(jax.random.key(seed), 10)
    return {
        "inputs": bell_draw(key_of[0], (CASES, ROWS, C, NX), 1.0, 6.0, ((0, 8), (1, 64))),
        "preact": bell_draw(key_of[1], (CASES, ROWS, C, NX), 1.0, 4.0, ((0, 8), (1, 64))),
        "spectral_weight": bell_draw(key_of[2], (KY, KX, C, 2 * C), 1.0, 6.0, ((0, 8), (1, 64))),
        "point_weight": bell_draw(key_of[3], (C, C), C ** -0.5, 0.75),
        "readout": bell_draw(key_of[4], (STEPS, 2, C), C ** -0.5, 0.75, (), jnp.float32),
        "observed": bell_draw(key_of[5], (CASES, 2, N_DOMAIN * SLOTS), 0.5, 4.0, ((0, 8), (2, 64)), jnp.float32),
        "cell_index": with_ends(jax.random.randint(key_of[6], (CASES, N_DOMAIN * SLOTS), 0, ROWS_DEV * NX), jax.random.fold_in(key_of[6], 1), 0, (ROWS_DEV * NX) - 1).astype(jnp.int32),
        "drift_steps": with_ends(jax.random.randint(key_of[7], (CASES, N_DOMAIN * SLOTS), 0, STEPS), jax.random.fold_in(key_of[7], 1), 0, STEPS - 1).astype(jnp.int32),
        "counts": draw_counts(jax.random.fold_in(key_of[9], 71), 0),
    }


two_pi = 6.283185307179586
loss_scale = 8.0

def gelu_fn(value):
    return jax.nn.gelu(value, approximate=True)

def lon_tables():
    wavenum = jnp.arange(KX, dtype=jnp.int32)
    points = jnp.arange(NX, dtype=jnp.int32)
    phase = (points[:, None] * wavenum[None, :] % NX).astype(jnp.float32) * (two_pi / NX)
    return (jnp.cos(phase).astype(jnp.bfloat16), (-jnp.sin(phase)).astype(jnp.bfloat16))

def lat_tables():
    index_q = jnp.arange(KY, dtype=jnp.int32)
    wavenum = jnp.where(index_q < KY // 2, index_q, NY - KY + index_q)
    rows_y = jnp.arange(ROWS, dtype=jnp.int32) * (NY // ROWS)
    phase = (wavenum[:, None] * rows_y[None, :] % NY).astype(jnp.float32) * (two_pi / NY)
    return (jnp.cos(phase).astype(jnp.bfloat16), jnp.sin(phase).astype(jnp.bfloat16))

def mix(table, field, form):
    return jnp.einsum(form, table.astype(jnp.float32), field.astype(jnp.float32))

def reference(inputs, preact, spectral_weight, point_weight, readout, observed, cell_index, drift_steps, counts):
    case_count = inputs.shape[0]
    lat_rows = ROWS // N_DOMAIN
    total = N_DOMAIN * SLOTS
    entry = jnp.arange(total, dtype=jnp.int32)
    slab_of = entry // SLOTS
    live = ((entry % SLOTS)[None, :] < counts[:, slab_of]).astype(jnp.float32)
    row_of = slab_of[None, :] * lat_rows + cell_index // NX
    col_of = cell_index % NX
    case_idx = jnp.broadcast_to(jnp.arange(case_count, dtype=jnp.int32)[:, None], cell_index.shape)
    zslot = preact[case_idx, row_of, :, col_of].astype(jnp.float32)
    onehot = (drift_steps[..., None] == jnp.arange(STEPS, dtype=jnp.int32)).astype(jnp.float32)
    chosen = jnp.einsum('nes,sjc->nejc', onehot, readout.astype(jnp.float32))
    activated, pullback = jax.vjp(gelu_fn, zslot)
    velocity = jnp.einsum('nejc,nec->nej', chosen, activated)
    misfit = loss_scale * live[..., None] * (velocity - jnp.transpose(observed, (0, 2, 1)))
    dact = jnp.einsum('nejc,nej->nec', chosen, misfit)
    dslot = pullback(dact)[0]
    dgrid = jnp.zeros(inputs.shape, jnp.float32).at[case_idx, row_of, :, col_of].add(dslot)
    dz = dgrid.astype(jnp.bfloat16)
    cos_x, nsin_x = lon_tables()
    cos_y, sin_y = lat_tables()

    def lon_forward(field):
        flat = field.reshape(-1, NX)
        real_part = jnp.dot(flat, cos_x, preferred_element_type=jnp.float32)
        imag_part = jnp.dot(flat, nsin_x, preferred_element_type=jnp.float32)
        shape = (case_count, ROWS, C, KX)
        return (real_part.astype(jnp.bfloat16).reshape(shape), imag_part.astype(jnp.bfloat16).reshape(shape))

    def lat_forward(real_part, imag_part):
        out_r = mix(cos_y, real_part, 'qy,nyck->nqck') + mix(sin_y, imag_part, 'qy,nyck->nqck')
        out_i = mix(cos_y, imag_part, 'qy,nyck->nqck') - mix(sin_y, real_part, 'qy,nyck->nqck')
        return (out_r, out_i)
    xa_r, xa_i = lon_forward(inputs)
    za_r, za_i = lon_forward(dz)
    xh_r, xh_i = lat_forward(xa_r, xa_i)
    xh_r = xh_r.astype(jnp.bfloat16)
    xh_i = xh_i.astype(jnp.bfloat16)
    wavenum = jnp.arange(KX, dtype=jnp.int32)
    mscale = jnp.where(wavenum == 0, 1.0, 2.0).astype(jnp.float32) / (NX * ROWS)
    dy_r, dy_i = lat_forward(za_r, za_i)
    dy_r = (dy_r * mscale).astype(jnp.bfloat16)
    dy_i = (dy_i * mscale).astype(jnp.bfloat16)
    w_r = spectral_weight[..., :C].astype(jnp.float32)
    w_i = spectral_weight[..., C:].astype(jnp.float32)
    fx_r, fx_i = (xh_r.astype(jnp.float32), xh_i.astype(jnp.float32))
    fy_r, fy_i = (dy_r.astype(jnp.float32), dy_i.astype(jnp.float32))
    gw_r = jnp.einsum('nqck,nqok->qkco', fx_r, fy_r) + jnp.einsum('nqck,nqok->qkco', fx_i, fy_i)
    gw_i = jnp.einsum('nqck,nqok->qkco', fx_r, fy_i) - jnp.einsum('nqck,nqok->qkco', fx_i, fy_r)
    weight_grad = jnp.concatenate([gw_r, gw_i], axis=-1).astype(jnp.bfloat16)
    dx_r = jnp.einsum('qkco,nqok->nqck', w_r, fy_r) + jnp.einsum('qkco,nqok->nqck', w_i, fy_i)
    dx_i = jnp.einsum('qkco,nqok->nqck', w_r, fy_i) - jnp.einsum('qkco,nqok->nqck', w_i, fy_r)
    dx_r = dx_r.astype(jnp.bfloat16)
    dx_i = dx_i.astype(jnp.bfloat16)
    g_r = (mix(cos_y, dx_r, 'qy,nqck->nyck') - mix(sin_y, dx_i, 'qy,nqck->nyck')).astype(jnp.bfloat16)
    g_i = (mix(cos_y, dx_i, 'qy,nqck->nyck') + mix(sin_y, dx_r, 'qy,nqck->nyck')).astype(jnp.bfloat16)
    point_f = point_weight.astype(jnp.float32)

    def one_case(index):
        part_r = g_r[index].reshape(-1, KX)
        part_i = g_i[index].reshape(-1, KX)
        spectral = jnp.dot(part_r, cos_x.T, preferred_element_type=jnp.float32)
        spectral = spectral + jnp.dot(part_i, nsin_x.T, preferred_element_type=jnp.float32)
        spectral = spectral.reshape(ROWS, C, NX)
        pointwise = jnp.einsum('yox,co->ycx', dz[index].astype(jnp.float32), point_f)
        return (spectral + pointwise).astype(jnp.bfloat16)
    input_grad = lax.map(one_case, jnp.arange(case_count, dtype=jnp.int32))
    return (input_grad, weight_grad)
```

```python
import numpy as np
import ml_dtypes
import jax
import jax.numpy as jnp
from jax import lax
from jax.experimental import pallas as pl
from jax.experimental.pallas import tpu as pltpu
from jax.sharding import PartitionSpec as P

NX = 2304
NY = 2160
KX = 256
KY = 128
STEPS = 48
SLOTS = 512
C = 64
ROWS_DEV = 3
N_DOMAIN = 64
N_DP = 8
ROWS = ROWS_DEV * N_DOMAIN
QL = KY // N_DP
LC = ROWS_DEV * C

two_pi = 6.283185307179586
loss_scale = 8.0
gelu_a = 0.7978845608
gelu_b = 0.044715

f32 = jnp.float32
bf16 = jnp.bfloat16


def lon_table():
    kl, part, kh, block = np.meshgrid(np.arange(2), np.arange(2), np.arange(2), np.arange(N_DOMAIN), indexing="ij")
    wavenum = (4 * block + 2 * kh + kl).reshape(-1, 1).astype(np.int64)
    part = part.reshape(-1, 1)
    phase = (wavenum * np.arange(NX)[None, :] % NX) * (two_pi / NX)
    return np.where(part == 0, np.cos(phase), -np.sin(phase)).astype(ml_dtypes.bfloat16)


def lat_table():
    block, part, ql = np.meshgrid(np.arange(N_DP), np.arange(2), np.arange(QL), indexing="ij")
    part2, l, slab = np.meshgrid(np.arange(2), np.arange(ROWS_DEV), np.arange(N_DOMAIN), indexing="ij")
    index_q = (block * QL + ql).reshape(-1, 1)
    wavenum = np.where(index_q < KY // 2, index_q, NY - KY + index_q).astype(np.int64)
    rows_y = (slab * ROWS_DEV + l).reshape(1, -1) * (NY // ROWS)
    phase = (wavenum * rows_y % NY) * (two_pi / NY)
    part, part2 = part.reshape(-1, 1), part2.reshape(1, -1)
    sine = np.where(part < part2, np.sin(phase), -np.sin(phase))
    return np.where(part == part2, np.cos(phase), sine).astype(ml_dtypes.bfloat16)


def dot(a, b, contract, precision=None):
    return lax.dot_general(a, b, ((contract[0], contract[1]), ((), ())), precision=precision, preferred_element_type=f32)


NN = ((1,), (0,))
NT = ((1,), (1,))
TN = ((0,), (0,))


def slots_kernel(x_ref, p_ref, t_ref, ro_ref, obs_ref, cell_ref, step_ref, cnt_ref, msg_ref, dz_ref, oh_ref, sc_ref):
    cell = cell_ref[...]
    row = (cell >= NX).astype(jnp.int32) + (cell >= 2 * NX).astype(jnp.int32)
    col = cell - row * NX
    for i in range(NX // 256):
        here = lax.broadcasted_iota(jnp.int32, (256, SLOTS), 0) + i * 256
        oh_ref[i * 256 : (i + 1) * 256, :] = (here == col).astype(f32).astype(bf16)
    zall = dot(p_ref[...], oh_ref[...], NN)
    z = jnp.zeros((C, SLOTS), f32)
    for l in range(ROWS_DEV):
        z = z + jnp.where(row == l, zall[l * C : (l + 1) * C], 0.0)
    step_hot = (lax.broadcasted_iota(jnp.int32, (STEPS, SLOTS), 0) == step_ref[...]).astype(f32)
    chosen = dot(ro_ref[...], step_hot, TN, lax.Precision.HIGHEST)
    th = jnp.tanh(gelu_a * (z + gelu_b * (z * z * z)))
    act = 0.5 * z * (1.0 + th)
    slope = 0.5 * (1.0 + th) + 0.5 * z * (1.0 - th * th) * (gelu_a * (1.0 + 3.0 * gelu_b * (z * z)))
    live = (lax.broadcasted_iota(jnp.int32, (1, SLOTS), 1) < cnt_ref[...]).astype(f32)
    back = jnp.zeros((C, SLOTS), f32)
    for j in range(2):
        cj = chosen[j * C : (j + 1) * C]
        velocity = jnp.sum(cj * act, axis=0, keepdims=True)
        back = back + cj * (loss_scale * live * (velocity - obs_ref[j : j + 1, :]))
    dslot = slope * back
    hi = dslot.astype(bf16).astype(f32)
    lo = dslot - hi
    zero = jnp.zeros((C, SLOTS), f32)
    spread = [jnp.where(row == l, part, zero).astype(bf16) for part in (hi, lo) for l in range(ROWS_DEV)]
    both = jnp.concatenate(spread, axis=0)
    step = 768
    for i in range(NX // step):
        grid = dot(both, oh_ref[i * step : (i + 1) * step, :], NT)
        dz_ref[:, i * step : (i + 1) * step] = (grid[:LC] + grid[LC:]).astype(bf16)
    for xz, field in enumerate((x_ref, dz_ref)):
        spec = dot(t_ref[...], field[...], NT)
        for l in range(ROWS_DEV):
            for pk in range(4):
                block = jnp.concatenate(
                    [spec[(kl * 4 + pk) * 64 : (kl * 4 + pk + 1) * 64, l * C : (l + 1) * C] for kl in range(2)], axis=1
                )
                sc_ref[l, pl.ds(xz * 4 + pk, N_DOMAIN, stride=8), :] = block
    for l in range(ROWS_DEV):
        msg_ref[:, :, l * 128 : (l + 1) * 128] = sc_ref[l].reshape(N_DOMAIN, 8, 128).astype(bf16)


def lat_kernel(msg_ref, m_ref, scale_ref, out_ref, sc_ref, rhs_ref):
    for l in range(ROWS_DEV):
        sc_ref[l] = msg_ref[:, :, l * 128 : (l + 1) * 128].astype(f32).reshape(N_DOMAIN * 8, 128)
    for xz in range(2):
        for part in range(2):
            for kh in range(2):
                for l in range(ROWS_DEV):
                    block = sc_ref[l, pl.ds(xz * 4 + part * 2 + kh, N_DOMAIN, stride=8), :]
                    at, lane = (part * ROWS_DEV + l) * N_DOMAIN, (xz * 2 + kh) * 128
                    rhs_ref[at : at + N_DOMAIN, lane : lane + 128] = block.astype(bf16)
    modes = dot(m_ref[...], rhs_ref[...], NN)
    for xz in range(2):
        for kh in range(2):
            b = xz * 2 + kh
            part = modes[:, b * 128 : (b + 1) * 128]
            if xz == 1:
                part = part * scale_ref[:, kh * 128 : (kh + 1) * 128]
            part = part.astype(bf16)
            for d in range(N_DP):
                out_ref[d, b * 32 : (b + 1) * 32, :] = part[d * 32 : (d + 1) * 32]


def load_modes(ref, kh, ql):
    re = ref[pl.ds(kh * 32 + ql, N_DP, stride=64), :]
    im = ref[pl.ds(kh * 32 + QL + ql, N_DP, stride=64), :]
    return re, im


def paired(re, im):
    top = jnp.concatenate([re, im], axis=1)
    low = jnp.concatenate([im, -re], axis=1)
    return jnp.concatenate([top, low], axis=0).astype(bf16)


def mix_kernel(modes_ref, w_ref, out_ref, y_ref, sc_ref):
    for n in range(N_DP):
        y_ref[n * 64 : (n + 1) * 64, :] = modes_ref[n, 64:128, :].astype(f32)
    zero = jnp.zeros((C, C), bf16)
    for kh in range(2):
        for ql in range(QL):
            lhs = paired(*load_modes(y_ref, kh, ql))
            w0, w1 = w_ref[ql, kh * 2], w_ref[ql, kh * 2 + 1]
            rhs = jnp.concatenate(
                [
                    jnp.concatenate([w0[:, :C], zero, w0[:, C:], zero], axis=1),
                    jnp.concatenate([zero, w1[:, :C], zero, w1[:, C:]], axis=1),
                ],
                axis=0,
            )
            back = dot(lhs, rhs, NT)
            sc_ref[pl.ds(kh * 32 + ql, N_DP, stride=64), :] = back[:N_DP]
            sc_ref[pl.ds(kh * 32 + QL + ql, N_DP, stride=64), :] = back[N_DP:]
    for n in range(N_DP):
        out_ref[n] = sc_ref[n * 64 : (n + 1) * 64, :].astype(bf16)


def weight_kernel(modes_ref, out_ref, x_ref, y_ref):
    for n in range(N_DP):
        x_ref[n * 64 : (n + 1) * 64, :] = modes_ref[n, 0:64, :].astype(f32)
        y_ref[n * 64 : (n + 1) * 64, :] = modes_ref[n, 64:128, :].astype(f32)
    for kh in range(2):
        for ql in range(QL):
            rhs = paired(*load_modes(y_ref, kh, ql))
            lhs = jnp.concatenate(load_modes(x_ref, kh, ql), axis=0).astype(bf16)
            grad = dot(lhs, rhs, TN)
            for kl in range(2):
                mine = grad[kl * C : (kl + 1) * C]
                re = mine[:, kl * C : (kl + 1) * C]
                im = mine[:, 128 + kl * C : 128 + (kl + 1) * C]
                out_ref[ql, kh * 2 + kl] = jnp.concatenate([re, im], axis=1).astype(bf16)


def synth_kernel(modes_ref, m_ref, out_ref, d_ref, sc_ref):
    for q in range(N_DP):
        for kh in range(2):
            d_ref[q * 32 : (q + 1) * 32, kh * 128 : (kh + 1) * 128] = modes_ref[q, kh * 32 : (kh + 1) * 32, :]
    lat = dot(m_ref[...], d_ref[...], NN)
    for part in range(2):
        for l in range(ROWS_DEV):
            at = (part * ROWS_DEV + l) * N_DOMAIN
            for kh in range(2):
                block = lat[at : at + N_DOMAIN, kh * 128 : (kh + 1) * 128]
                sc_ref[l, pl.ds(part * 2 + kh, N_DOMAIN, stride=4), :] = block
    for l in range(ROWS_DEV):
        out_ref[:, :, l * 128 : (l + 1) * 128] = sc_ref[l].reshape(N_DOMAIN, 4, 128).astype(bf16)


def grad_kernel(msg_ref, t_ref, dz_ref, pw_ref, out_ref, sc_ref, lhs_ref, pd_ref):
    for l in range(ROWS_DEV):
        sc_ref[l] = msg_ref[:, :, l * 128 : (l + 1) * 128].astype(f32).reshape(N_DOMAIN * 4, 128)
    pd_ref[...] = jnp.zeros((LC, LC), bf16)
    for l in range(ROWS_DEV):
        blocks = [sc_ref[l, pl.ds(pk, N_DOMAIN, stride=4), :] for pk in range(4)]
        turned = jnp.concatenate(blocks, axis=0).T
        for kl in range(2):
            lhs_ref[l * C : (l + 1) * C, kl * 256 : (kl + 1) * 256] = turned[kl * C : (kl + 1) * C].astype(bf16)
        pd_ref[l * C : (l + 1) * C, l * C : (l + 1) * C] = pw_ref[...]
    step = 768
    for i in range(NX // step):
        cols = slice(i * step, (i + 1) * step)
        out = dot(lhs_ref[...], t_ref[:, cols], NN) + dot(pd_ref[...], dz_ref[:, cols], NN)
        out_ref[:, cols] = out.astype(bf16)


def call(kernel, outs, scratch, flops, *args):
    whole = pl.BlockSpec(memory_space=pltpu.VMEM)
    nbytes = sum(a.size * a.dtype.itemsize for a in args)
    return pl.pallas_call(
        kernel,
        out_shape=outs,
        in_specs=[whole] * len(args),
        out_specs=jax.tree.map(lambda _: whole, outs),
        scratch_shapes=scratch,
        cost_estimate=pl.CostEstimate(flops=flops, bytes_accessed=nbytes, transcendentals=0),
        compiler_params=pltpu.CompilerParams(vmem_limit_bytes=40 * 1024 * 1024),
    )(*args)


def local(inputs, preact, spectral_weight, point_weight, readout, observed, cell_index, drift_steps, counts):
    table = jnp.asarray(lon_table())
    lat = lat_table()
    m_fwd, m_inv = jnp.asarray(lat), jnp.asarray(np.ascontiguousarray(lat.T))
    first = (lax.axis_index("domain") == 0) & (jnp.arange(256) < C)
    scale = jnp.where(first, 1.0, 2.0).astype(f32)[None, :] / (NX * ROWS)

    msg, dz = call(
        slots_kernel,
        (
            jax.ShapeDtypeStruct((N_DOMAIN, 8, 384), bf16),
            jax.ShapeDtypeStruct((LC, NX), bf16),
        ),
        [pltpu.VMEM((NX, SLOTS), bf16), pltpu.VMEM((ROWS_DEV, 512, 128), f32)],
        2 * LC * NX * 512 * 5,
        inputs.reshape(LC, NX),
        preact.reshape(LC, NX),
        table,
        readout.reshape(STEPS, 2 * C),
        observed.reshape(2, SLOTS),
        cell_index,
        drift_steps,
        counts,
    )
    msg = lax.all_to_all(msg, "domain", 0, 0, tiled=True)
    modes = call(
        lat_kernel,
        jax.ShapeDtypeStruct((N_DP, 128, 128), bf16),
        [pltpu.VMEM((ROWS_DEV, 512, 128), f32), pltpu.VMEM((384, 512), bf16)],
        2 * 256 * 384 * 512,
        msg,
        m_fwd,
        scale,
    )
    modes = lax.all_to_all(modes, "dp", 0, 0, tiled=True)
    dmodes = call(
        mix_kernel,
        jax.ShapeDtypeStruct((N_DP, 64, 128), bf16),
        [pltpu.VMEM((512, 128), f32), pltpu.VMEM((512, 128), f32)],
        2 * 32 * 128 * 128 * 256,
        modes,
        spectral_weight,
    )
    dmodes = lax.all_to_all(dmodes, "dp", 0, 0, tiled=True)
    weight_grad = call(
        weight_kernel,
        jax.ShapeDtypeStruct((QL, 4, C, 2 * C), bf16),
        [pltpu.VMEM((512, 128), f32), pltpu.VMEM((512, 128), f32)],
        2 * 32 * 128 * 128 * 256,
        modes,
    )
    msg = call(
        synth_kernel,
        jax.ShapeDtypeStruct((N_DOMAIN, 4, 384), bf16),
        [pltpu.VMEM((256, 256), bf16), pltpu.VMEM((ROWS_DEV, 256, 128), f32)],
        2 * 256 * 384 * 256,
        dmodes,
        m_inv,
    )
    msg = lax.all_to_all(msg, "domain", 0, 0, tiled=True)
    input_grad = call(
        grad_kernel,
        jax.ShapeDtypeStruct((LC, NX), bf16),
        [pltpu.VMEM((ROWS_DEV, 256, 128), f32), pltpu.VMEM((LC, 512), bf16), pltpu.VMEM((LC, LC), bf16)],
        2 * LC * NX * 704,
        msg,
        table,
        dz,
        point_weight,
    )
    return (input_grad.reshape(1, ROWS_DEV, C, NX), weight_grad)


def solution(mesh):
    placed = (
        P("dp", "domain", None, None),
        P("dp", "domain", None, None),
        P("dp", "domain", None, None),
        P(),
        P(),
        P("dp", None, "domain"),
        P("dp", "domain"),
        P("dp", "domain"),
        P("dp", "domain"),
    )
    return jax.shard_map(
        local,
        mesh=mesh,
        in_specs=placed,
        out_specs=(P("dp", "domain", None, None), P("dp", "domain", None, None)),
        check_vma=False,
    )
```

```python
import numpy as np
import ml_dtypes
import jax
import jax.numpy as jnp
from jax import lax
from jax.experimental import pallas as pl
from jax.experimental.pallas import tpu as pltpu
from jax.sharding import PartitionSpec as P

NX = 2304
NY = 2160
KX = 256
KY = 128
STEPS = 48
SLOTS = 512
C = 64
ROWS_DEV = 3
N_DOMAIN = 64
N_DP = 8
ROWS = ROWS_DEV * N_DOMAIN
QL = KY // N_DP
LC = ROWS_DEV * C

two_pi = 6.283185307179586
loss_scale = 8.0
gelu_a = 0.7978845608
gelu_b = 0.044715

f32 = jnp.float32
bf16 = jnp.bfloat16


def lon_table():
    kl, part, kh, block = np.meshgrid(np.arange(2), np.arange(2), np.arange(2), np.arange(N_DOMAIN), indexing="ij")
    wavenum = (4 * block + 2 * kh + kl).reshape(-1, 1).astype(np.int64)
    part = part.reshape(-1, 1)
    phase = (wavenum * np.arange(NX)[None, :] % NX) * (two_pi / NX)
    return np.where(part == 0, np.cos(phase), -np.sin(phase)).astype(ml_dtypes.bfloat16)


def lat_table():
    block, part, ql = np.meshgrid(np.arange(N_DP), np.arange(2), np.arange(QL), indexing="ij")
    part2, l, slab = np.meshgrid(np.arange(2), np.arange(ROWS_DEV), np.arange(N_DOMAIN), indexing="ij")
    index_q = (block * QL + ql).reshape(-1, 1)
    wavenum = np.where(index_q < KY // 2, index_q, NY - KY + index_q).astype(np.int64)
    rows_y = (slab * ROWS_DEV + l).reshape(1, -1) * (NY // ROWS)
    phase = (wavenum * rows_y % NY) * (two_pi / NY)
    part, part2 = part.reshape(-1, 1), part2.reshape(1, -1)
    sine = np.where(part < part2, np.sin(phase), -np.sin(phase))
    return np.where(part == part2, np.cos(phase), sine).astype(ml_dtypes.bfloat16)


def dot(a, b, contract, precision=None):
    return lax.dot_general(a, b, ((contract[0], contract[1]), ((), ())), precision=precision, preferred_element_type=f32)


NN = ((1,), (0,))
NT = ((1,), (1,))
TN = ((0,), (0,))


def slots_kernel(
    x_hbm, p_hbm, t_hbm, ro_hbm, obs_hbm, cell_hbm, step_hbm, cnt_ref, msg_hbm, dz_hbm,
    msg_ref, dz_ref, oh_ref, sc_ref, x_ref, p_ref, t_ref, ro_ref, obs_ref, cell_ref, step_ref, sems, out_sems,
):
    moves = (
        (cell_hbm, cell_ref),
        (step_hbm, step_ref),
        (obs_hbm, obs_ref),
        (ro_hbm, ro_ref),
        (p_hbm, p_ref),
        (t_hbm, t_ref),
        (x_hbm, x_ref),
    )
    copies = [pltpu.make_async_copy(src, dst, sems.at[i]) for i, (src, dst) in enumerate(moves)]
    for copy in copies:
        copy.start()
    copies[0].wait()
    cell = cell_ref[...]
    row = (cell >= NX).astype(jnp.int32) + (cell >= 2 * NX).astype(jnp.int32)
    col = cell - row * NX
    for i in range(NX // 256):
        here = lax.broadcasted_iota(jnp.int32, (256, SLOTS), 0) + i * 256
        oh_ref[i * 256 : (i + 1) * 256, :] = (here == col).astype(f32).astype(bf16)
    for copy in copies[1:5]:
        copy.wait()
    zall = dot(p_ref[...], oh_ref[...], NN)
    z = jnp.zeros((C, SLOTS), f32)
    for l in range(ROWS_DEV):
        z = z + jnp.where(row == l, zall[l * C : (l + 1) * C], 0.0)
    step_hot = (lax.broadcasted_iota(jnp.int32, (STEPS, SLOTS), 0) == step_ref[...]).astype(f32)
    chosen = [dot(ro_ref[:, j, :], step_hot, TN, lax.Precision.HIGHEST) for j in range(2)]
    th = jnp.tanh(gelu_a * (z + gelu_b * (z * z * z)))
    act = 0.5 * z * (1.0 + th)
    slope = 0.5 * (1.0 + th) + 0.5 * z * (1.0 - th * th) * (gelu_a * (1.0 + 3.0 * gelu_b * (z * z)))
    live = (lax.broadcasted_iota(jnp.int32, (1, SLOTS), 1) < cnt_ref[0, 0]).astype(f32)
    back = jnp.zeros((C, SLOTS), f32)
    for j in range(2):
        cj = chosen[j]
        velocity = jnp.sum(cj * act, axis=0, keepdims=True)
        back = back + cj * (loss_scale * live * (velocity - obs_ref[j : j + 1, :]))
    dslot = slope * back
    hi = dslot.astype(bf16).astype(f32)
    lo = dslot - hi
    zero = jnp.zeros((C, SLOTS), f32)
    spread = [jnp.where(row == l, part, zero).astype(bf16) for part in (hi, lo) for l in range(ROWS_DEV)]
    both = jnp.concatenate(spread, axis=0)
    step = 768
    outs = []
    for i in range(NX // step):
        grid = dot(both, oh_ref[i * step : (i + 1) * step, :], NT)
        cols = slice(i * step, (i + 1) * step)
        dz_ref[:, cols] = (grid[:LC] + grid[LC:]).astype(bf16)
        outs.append(pltpu.make_async_copy(dz_ref.at[:, cols], dz_hbm.at[:, cols], out_sems.at[i]))
        outs[-1].start()
    copies[5].wait()
    copies[6].wait()
    for xz, field in enumerate((x_ref, dz_ref)):
        spec = dot(t_ref[...], field[...], NT)
        for l in range(ROWS_DEV):
            for pk in range(4):
                block = jnp.concatenate(
                    [spec[(kl * 4 + pk) * 64 : (kl * 4 + pk + 1) * 64, l * C : (l + 1) * C] for kl in range(2)], axis=1
                )
                sc_ref[l, pl.ds(xz * 4 + pk, N_DOMAIN, stride=8), :] = block
    for l in range(ROWS_DEV):
        lanes = slice(l * 128, (l + 1) * 128)
        msg_ref[:, :, lanes] = sc_ref[l].reshape(N_DOMAIN, 8, 128).astype(bf16)
        outs.append(pltpu.make_async_copy(msg_ref.at[:, :, lanes], msg_hbm.at[:, :, lanes], out_sems.at[3 + l]))
        outs[-1].start()
    for copy in outs:
        copy.wait()


def lat_kernel(msg_ref, m_ref, w_ref, out_ref, w_out_ref, m_out_ref, sc_ref, rhs_ref):
    w_out_ref[...] = w_ref[...]
    m_out_ref[...] = m_ref[...]
    for l in range(ROWS_DEV):
        sc_ref[l] = msg_ref[:, :, l * 128 : (l + 1) * 128].astype(f32).reshape(N_DOMAIN * 8, 128)
    for xz in range(2):
        for part in range(2):
            for kh in range(2):
                for l in range(ROWS_DEV):
                    block = sc_ref[l, pl.ds(xz * 4 + part * 2 + kh, N_DOMAIN, stride=8), :]
                    at, lane = (part * ROWS_DEV + l) * N_DOMAIN, (xz * 2 + kh) * 128
                    rhs_ref[at : at + N_DOMAIN, lane : lane + 128] = block.astype(bf16)
    lead = (lax.axis_index("domain") == 0) & (lax.broadcasted_iota(jnp.int32, (1, 256), 1) < C)
    scale = jnp.where(lead, 1.0 / (NX * ROWS), 2.0 / (NX * ROWS))
    modes = dot(m_ref[...], rhs_ref[...], NN)
    for xz in range(2):
        for kh in range(2):
            b = xz * 2 + kh
            part = modes[:, b * 128 : (b + 1) * 128]
            if xz == 1:
                part = part * scale[:, kh * 128 : (kh + 1) * 128]
            part = part.astype(bf16)
            for d in range(N_DP):
                out_ref[d, b * 32 : (b + 1) * 32, :] = part[d * 32 : (d + 1) * 32]


def load_modes(ref, kh, ql):
    re = ref[pl.ds(kh * 32 + ql, N_DP, stride=64), :]
    im = ref[pl.ds(kh * 32 + QL + ql, N_DP, stride=64), :]
    return re, im


def paired(re, im):
    top = jnp.concatenate([re, im], axis=1)
    low = jnp.concatenate([im, -re], axis=1)
    return jnp.concatenate([top, low], axis=0).astype(bf16)


def mix_kernel(modes_ref, w_ref, m_ref, out_ref, m_out_ref, y_ref, sc_ref):
    m_out_ref[...] = m_ref[...]
    for n in range(N_DP):
        y_ref[n * 64 : (n + 1) * 64, :] = modes_ref[n, 64:128, :].astype(f32)
    zero = jnp.zeros((C, C), bf16)
    for kh in range(2):
        for ql in range(QL):
            lhs = paired(*load_modes(y_ref, kh, ql))
            w0, w1 = w_ref[ql, kh * 2], w_ref[ql, kh * 2 + 1]
            rhs = jnp.concatenate(
                [
                    jnp.concatenate([w0[:, :C], zero, w0[:, C:], zero], axis=1),
                    jnp.concatenate([zero, w1[:, :C], zero, w1[:, C:]], axis=1),
                ],
                axis=0,
            )
            back = dot(lhs, rhs, NT)
            sc_ref[pl.ds(kh * 32 + ql, N_DP, stride=64), :] = back[:N_DP]
            sc_ref[pl.ds(kh * 32 + QL + ql, N_DP, stride=64), :] = back[N_DP:]
    for n in range(N_DP):
        out_ref[n] = sc_ref[n * 64 : (n + 1) * 64, :].astype(bf16)


def weight_kernel(modes_ref, out_ref, x_ref, y_ref):
    for n in range(N_DP):
        x_ref[n * 64 : (n + 1) * 64, :] = modes_ref[n, 0:64, :].astype(f32)
        y_ref[n * 64 : (n + 1) * 64, :] = modes_ref[n, 64:128, :].astype(f32)
    for kh in range(2):
        for ql in range(QL):
            rhs = paired(*load_modes(y_ref, kh, ql))
            lhs = jnp.concatenate(load_modes(x_ref, kh, ql), axis=0).astype(bf16)
            grad = dot(lhs, rhs, TN)
            for kl in range(2):
                mine = grad[kl * C : (kl + 1) * C]
                re = mine[:, kl * C : (kl + 1) * C]
                im = mine[:, 128 + kl * C : 128 + (kl + 1) * C]
                out_ref[ql, kh * 2 + kl] = jnp.concatenate([re, im], axis=1).astype(bf16)


def synth_kernel(modes_ref, m_ref, out_ref, d_ref, sc_ref):
    for q in range(N_DP):
        for kh in range(2):
            d_ref[q * 32 : (q + 1) * 32, kh * 128 : (kh + 1) * 128] = modes_ref[q, kh * 32 : (kh + 1) * 32, :]
    lat = dot(m_ref[...], d_ref[...], TN)
    for part in range(2):
        for l in range(ROWS_DEV):
            at = (part * ROWS_DEV + l) * N_DOMAIN
            for kh in range(2):
                block = lat[at : at + N_DOMAIN, kh * 128 : (kh + 1) * 128]
                sc_ref[l, pl.ds(part * 2 + kh, N_DOMAIN, stride=4), :] = block
    for l in range(ROWS_DEV):
        out_ref[:, :, l * 128 : (l + 1) * 128] = sc_ref[l].reshape(N_DOMAIN, 4, 128).astype(bf16)


def grad_kernel(msg_ref, t_ref, dz_ref, pw_ref, out_hbm, sc_ref, lhs_ref, pd_ref, out_ref, sems):
    for l in range(ROWS_DEV):
        sc_ref[l] = msg_ref[:, :, l * 128 : (l + 1) * 128].astype(f32).reshape(N_DOMAIN * 4, 128)
    pd_ref[...] = jnp.zeros((LC, LC), bf16)
    for l in range(ROWS_DEV):
        blocks = [sc_ref[l, pl.ds(pk, N_DOMAIN, stride=4), :] for pk in range(4)]
        turned = jnp.concatenate(blocks, axis=0).T
        for kl in range(2):
            lhs_ref[l * C : (l + 1) * C, kl * 256 : (kl + 1) * 256] = turned[kl * C : (kl + 1) * C].astype(bf16)
        pd_ref[l * C : (l + 1) * C, l * C : (l + 1) * C] = pw_ref[...]
    step = 768
    copies = []
    for i in range(NX // step):
        cols = slice(i * step, (i + 1) * step)
        out = dot(lhs_ref[...], t_ref[:, cols], NN) + dot(pd_ref[...], dz_ref[:, cols], NN)
        out_ref[:, cols] = out.astype(bf16)
        copies.append(pltpu.make_async_copy(out_ref.at[:, cols], out_hbm.at[:, cols], sems.at[i]))
        copies[-1].start()
    for copy in copies:
        copy.wait()


WHOLE = pl.BlockSpec(memory_space=pltpu.VMEM)
FAR = pl.BlockSpec(memory_space=pltpu.HBM)


def call(kernel, outs, scratch, flops, *args, specs=None, out_specs=None, vmem=40):
    nbytes = sum(a.size * a.dtype.itemsize for a in args)
    return pl.pallas_call(
        kernel,
        out_shape=outs,
        in_specs=specs or [WHOLE] * len(args),
        out_specs=jax.tree.map(lambda _: WHOLE, outs) if out_specs is None else out_specs,
        scratch_shapes=scratch,
        cost_estimate=pl.CostEstimate(flops=flops, bytes_accessed=nbytes, transcendentals=0),
        compiler_params=pltpu.CompilerParams(vmem_limit_bytes=vmem * 1024 * 1024),
    )(*args)


def slots_call(inputs, preact, table, readout, observed, cell_index, drift_steps, counts):
    small = [pltpu.VMEM((1, SLOTS), jnp.int32), pltpu.VMEM((1, SLOTS), jnp.int32)]
    return call(
        slots_kernel,
        (
            jax.ShapeDtypeStruct((N_DOMAIN, 8, 384), bf16),
            jax.ShapeDtypeStruct((LC, NX), bf16),
        ),
        [
            pltpu.VMEM((N_DOMAIN, 8, 384), bf16),
            pltpu.VMEM((LC, NX), bf16),
            pltpu.VMEM((NX, SLOTS), bf16),
            pltpu.VMEM((ROWS_DEV, 512, 128), f32),
            pltpu.VMEM((LC, NX), bf16),
            pltpu.VMEM((LC, NX), bf16),
            pltpu.VMEM((512, NX), bf16),
            pltpu.VMEM((STEPS, 2, C), f32),
            pltpu.VMEM((2, SLOTS), f32),
            *small,
            pltpu.SemaphoreType.DMA((7,)),
            pltpu.SemaphoreType.DMA((6,)),
        ],
        2 * LC * NX * 512 * 5,
        inputs.reshape(LC, NX),
        preact.reshape(LC, NX),
        table,
        readout,
        observed.reshape(2, SLOTS),
        cell_index,
        drift_steps,
        counts,
        specs=[FAR] * 7 + [pl.BlockSpec(memory_space=pltpu.SMEM)],
        out_specs=(FAR, FAR),
        vmem=59,
    )


def local(inputs, preact, spectral_weight, point_weight, readout, observed, cell_index, drift_steps, counts):
    table = jnp.asarray(lon_table())
    lat = jnp.asarray(lat_table())
    msg, dz = slots_call(inputs, preact, table, readout, observed, cell_index, drift_steps, counts)
    msg = lax.all_to_all(msg, "domain", 0, 0, tiled=True)
    modes, weight, lat = call(
        lat_kernel,
        (
            jax.ShapeDtypeStruct((N_DP, 128, 128), bf16),
            jax.ShapeDtypeStruct((QL, 4, C, 2 * C), bf16),
            jax.ShapeDtypeStruct(lat.shape, bf16),
        ),
        [pltpu.VMEM((ROWS_DEV, 512, 128), f32), pltpu.VMEM((384, 512), bf16)],
        2 * 256 * 384 * 512,
        msg,
        lat,
        spectral_weight,
    )
    modes = lax.all_to_all(modes, "dp", 0, 0, tiled=True)
    dmodes, lat = call(
        mix_kernel,
        (jax.ShapeDtypeStruct((N_DP, 64, 128), bf16), jax.ShapeDtypeStruct(lat.shape, bf16)),
        [pltpu.VMEM((512, 128), f32), pltpu.VMEM((512, 128), f32)],
        2 * 32 * 128 * 128 * 256,
        modes,
        weight,
        lat,
    )
    dmodes = lax.all_to_all(dmodes, "dp", 0, 0, tiled=True)
    weight_grad = call(
        weight_kernel,
        jax.ShapeDtypeStruct((QL, 4, C, 2 * C), bf16),
        [pltpu.VMEM((512, 128), f32), pltpu.VMEM((512, 128), f32)],
        2 * 32 * 128 * 128 * 256,
        modes,
    )
    msg = call(
        synth_kernel,
        jax.ShapeDtypeStruct((N_DOMAIN, 4, 384), bf16),
        [
            pltpu.VMEM((256, 256), bf16),
            pltpu.VMEM((ROWS_DEV, 256, 128), f32),
        ],
        2 * 256 * 384 * 256,
        dmodes,
        lat,
    )
    msg = lax.all_to_all(msg, "domain", 0, 0, tiled=True)
    input_grad = call(
        grad_kernel,
        jax.ShapeDtypeStruct((LC, NX), bf16),
        [
            pltpu.VMEM((ROWS_DEV, 256, 128), f32),
            pltpu.VMEM((LC, 512), bf16),
            pltpu.VMEM((LC, LC), bf16),
            pltpu.VMEM((LC, NX), bf16),
            pltpu.SemaphoreType.DMA((3,)),
        ],
        2 * LC * NX * 704,
        msg,
        table,
        dz,
        point_weight,
        out_specs=FAR,
    )
    return (input_grad.reshape(1, ROWS_DEV, C, NX), weight_grad)


def solution(mesh):
    placed = (
        P("dp", "domain", None, None),
        P("dp", "domain", None, None),
        P("dp", "domain", None, None),
        P(),
        P(),
        P("dp", None, "domain"),
        P("dp", "domain"),
        P("dp", "domain"),
        P("dp", "domain"),
    )
    return jax.shard_map(
        local,
        mesh=mesh,
        in_specs=placed,
        out_specs=(P("dp", "domain", None, None), P("dp", "domain", None, None)),
        check_vma=False,
    )
```

```python
import numpy as np
import ml_dtypes
import jax
import jax.numpy as jnp
from jax import lax
from jax.experimental import pallas as pl
from jax.experimental.pallas import tpu as pltpu
from jax.sharding import PartitionSpec as P

NX = 2304
NY = 2160
KX = 256
KY = 128
STEPS = 48
SLOTS = 512
C = 64
ROWS_DEV = 3
N_DOMAIN = 64
N_DP = 8
ROWS = ROWS_DEV * N_DOMAIN
QL = KY // N_DP
LC = ROWS_DEV * C
HALF = NX // 2

two_pi = 6.283185307179586
loss_scale = 8.0
gelu_a = 0.7978845608
gelu_b = 0.044715

f32 = jnp.float32
bf16 = jnp.bfloat16


def lon_table():
    kl, part, kh, block = np.meshgrid(np.arange(2), np.arange(2), np.arange(2), np.arange(N_DOMAIN), indexing="ij")
    wavenum = (4 * block + 2 * kh + kl).reshape(-1, 1).astype(np.int64)
    part = part.reshape(-1, 1)
    phase = (wavenum * np.arange(HALF)[None, :] % NX) * (two_pi / NX)
    return np.where(part == 0, np.cos(phase), -np.sin(phase)).astype(ml_dtypes.bfloat16)


def lat_table():
    block, part, ql = np.meshgrid(np.arange(N_DP), np.arange(2), np.arange(QL), indexing="ij")
    part2, l, slab = np.meshgrid(np.arange(2), np.arange(ROWS_DEV), np.arange(N_DOMAIN), indexing="ij")
    index_q = (block * QL + ql).reshape(-1, 1)
    wavenum = np.where(index_q < KY // 2, index_q, NY - KY + index_q).astype(np.int64)
    rows_y = (slab * ROWS_DEV + l).reshape(1, -1) * (NY // ROWS)
    phase = (wavenum * rows_y % NY) * (two_pi / NY)
    part, part2 = part.reshape(-1, 1), part2.reshape(1, -1)
    sine = np.where(part < part2, np.sin(phase), -np.sin(phase))
    return np.where(part == part2, np.cos(phase), sine).astype(ml_dtypes.bfloat16)


def dot(a, b, contract, precision=None):
    return lax.dot_general(a, b, ((contract[0], contract[1]), ((), ())), precision=precision, preferred_element_type=f32)


NN = ((1,), (0,))
NT = ((1,), (1,))
TN = ((0,), (0,))


def where_slots(cell_ref):
    cell = cell_ref[...]
    row = (cell >= NX).astype(jnp.int32) + (cell >= 2 * NX).astype(jnp.int32)
    return row, cell - row * NX


def hot_slots(col, oh_ref):
    step = 128
    for i in range(oh_ref.shape[0] // step):
        here = lax.broadcasted_iota(jnp.int32, (step, SLOTS), 0) + i * step
        oh_ref[i * step : (i + 1) * step, :] = (here == col).astype(f32).astype(bf16)


def spread_slots(row, dslot):
    hi = dslot.astype(bf16).astype(f32)
    lo = dslot - hi
    zero = jnp.zeros((C, SLOTS), f32)
    return [
        jnp.concatenate([jnp.where(row == l, part, zero).astype(bf16) for l in range(ROWS_DEV)], axis=0)
        for part in (hi, lo)
    ]


def slots_kernel(
    x_hbm, p_hbm, t_hbm, ro_hbm, obs_hbm, cell_hbm, step_hbm, cnt_ref, msg_hbm, dslot_hbm,
    msg_ref, dslot_ref, oh_ref, sc_ref, x_ref, p_ref, t_ref, ro_ref, obs_ref, cell_ref, step_ref, sems, out_sems,
):
    moves = (
        (cell_hbm, cell_ref),
        (step_hbm, step_ref),
        (obs_hbm, obs_ref),
        (ro_hbm, ro_ref),
        (p_hbm.at[:, :HALF], p_ref.at[:LC]),
        (p_hbm.at[:, HALF:], p_ref.at[LC:]),
        (t_hbm, t_ref),
        (x_hbm, x_ref),
    )
    copies = [pltpu.make_async_copy(src, dst, sems.at[i]) for i, (src, dst) in enumerate(moves)]
    for copy in copies:
        copy.start()
    copies[0].wait()
    row, col = where_slots(cell_ref)
    east = (col >= HALF).astype(jnp.int32)
    hot_slots(col - east * HALF, oh_ref)
    place = east * ROWS_DEV + row
    for copy in copies[1:6]:
        copy.wait()
    zall = dot(p_ref[...], oh_ref[...], NN)
    z = jnp.zeros((C, SLOTS), f32)
    for i in range(2 * ROWS_DEV):
        z = z + jnp.where(place == i, zall[i * C : (i + 1) * C], 0.0)
    copies[6].wait()
    west = dot(t_ref[:256], oh_ref[...], NN).astype(bf16)
    turn = (1 - 2 * east).astype(f32)
    rest = (dot(t_ref[256:], oh_ref[...], NN) * turn).astype(bf16)
    step_hot = (lax.broadcasted_iota(jnp.int32, (STEPS, SLOTS), 0) == step_ref[...]).astype(f32)
    chosen = [dot(ro_ref[:, j, :], step_hot, TN, lax.Precision.HIGHEST) for j in range(2)]
    th = jnp.tanh(gelu_a * (z + gelu_b * (z * z * z)))
    act = 0.5 * z * (1.0 + th)
    slope = 0.5 * (1.0 + th) + 0.5 * z * (1.0 - th * th) * (gelu_a * (1.0 + 3.0 * gelu_b * (z * z)))
    live = (lax.broadcasted_iota(jnp.int32, (1, SLOTS), 1) < cnt_ref[0, 0]).astype(f32)
    back = jnp.zeros((C, SLOTS), f32)
    for j in range(2):
        cj = chosen[j]
        velocity = jnp.sum(cj * act, axis=0, keepdims=True)
        back = back + cj * (loss_scale * live * (velocity - obs_ref[j : j + 1, :]))
    dslot = slope * back
    dslot_ref[...] = dslot
    outs = [pltpu.make_async_copy(dslot_ref, dslot_hbm, out_sems.at[3])]
    outs[0].start()

    def place_spectra(xz, even, odd):
        for l in range(ROWS_DEV):
            for pk in range(4):
                block = jnp.concatenate(
                    [spec[pk * 64 : (pk + 1) * 64, l * C : (l + 1) * C] for spec in (even, odd)], axis=1
                )
                sc_ref[l, pl.ds(xz * 4 + pk, N_DOMAIN, stride=8), :] = block

    hi, lo = spread_slots(row, dslot)
    place_spectra(1, dot(west, hi, NT) + dot(west, lo, NT), dot(rest, hi, NT) + dot(rest, lo, NT))
    copies[7].wait()
    near, far = x_ref[:, :HALF].astype(f32), x_ref[:, HALF:].astype(f32)
    place_spectra(
        0, dot(t_ref[:256], (near + far).astype(bf16), NT), dot(t_ref[256:], (near - far).astype(bf16), NT)
    )
    for l in range(ROWS_DEV):
        lanes = slice(l * 128, (l + 1) * 128)
        msg_ref[:, :, lanes] = sc_ref[l].reshape(N_DOMAIN, 8, 128).astype(bf16)
        outs.append(pltpu.make_async_copy(msg_ref.at[:, :, lanes], msg_hbm.at[:, :, lanes], out_sems.at[l]))
        outs[-1].start()
    for copy in outs:
        copy.wait()


def scatter_kernel(dslot_ref, cell_ref, dz_ref, oh_ref):
    row, col = where_slots(cell_ref)
    hot_slots(col, oh_ref)
    both = jnp.concatenate(spread_slots(row, dslot_ref[...]), axis=0)
    step = 768
    for i in range(NX // step):
        grid = dot(both, oh_ref[i * step : (i + 1) * step, :], NT)
        dz_ref[:, i * step : (i + 1) * step] = (grid[:LC] + grid[LC:]).astype(bf16)


def lat_kernel(msg_ref, m_ref, w_ref, out_ref, w_out_ref, m_out_ref, sc_ref, rhs_ref):
    w_out_ref[...] = w_ref[...]
    m_out_ref[...] = m_ref[...]
    for l in range(ROWS_DEV):
        sc_ref[l] = msg_ref[:, :, l * 128 : (l + 1) * 128].astype(f32).reshape(N_DOMAIN * 8, 128)
    for xz in range(2):
        for part in range(2):
            for kh in range(2):
                for l in range(ROWS_DEV):
                    block = sc_ref[l, pl.ds(xz * 4 + part * 2 + kh, N_DOMAIN, stride=8), :]
                    at, lane = (part * ROWS_DEV + l) * N_DOMAIN, (xz * 2 + kh) * 128
                    rhs_ref[at : at + N_DOMAIN, lane : lane + 128] = block.astype(bf16)
    lead = (lax.axis_index("domain") == 0) & (lax.broadcasted_iota(jnp.int32, (1, 256), 1) < C)
    scale = jnp.where(lead, 1.0 / (NX * ROWS), 2.0 / (NX * ROWS))
    modes = dot(m_ref[...], rhs_ref[...], NN)
    for xz in range(2):
        for kh in range(2):
            b = xz * 2 + kh
            part = modes[:, b * 128 : (b + 1) * 128]
            if xz == 1:
                part = part * scale[:, kh * 128 : (kh + 1) * 128]
            part = part.astype(bf16)
            for d in range(N_DP):
                out_ref[d, b * 32 : (b + 1) * 32, :] = part[d * 32 : (d + 1) * 32]


def load_modes(ref, kh, ql):
    re = ref[pl.ds(kh * 32 + ql, N_DP, stride=64), :]
    im = ref[pl.ds(kh * 32 + QL + ql, N_DP, stride=64), :]
    return re, im


def paired(re, im):
    top = jnp.concatenate([re, im], axis=1)
    low = jnp.concatenate([im, -re], axis=1)
    return jnp.concatenate([top, low], axis=0).astype(bf16)


def mix_kernel(modes_ref, w_ref, m_ref, out_ref, m_out_ref, y_ref, sc_ref):
    m_out_ref[...] = m_ref[...]
    for n in range(N_DP):
        y_ref[n * 64 : (n + 1) * 64, :] = modes_ref[n, 64:128, :].astype(f32)
    zero = jnp.zeros((C, C), bf16)
    for kh in range(2):
        for ql in range(QL):
            lhs = paired(*load_modes(y_ref, kh, ql))
            w0, w1 = w_ref[ql, kh * 2], w_ref[ql, kh * 2 + 1]
            rhs = jnp.concatenate(
                [
                    jnp.concatenate([w0[:, :C], zero, w0[:, C:], zero], axis=1),
                    jnp.concatenate([zero, w1[:, :C], zero, w1[:, C:]], axis=1),
                ],
                axis=0,
            )
            back = dot(lhs, rhs, NT)
            sc_ref[pl.ds(kh * 32 + ql, N_DP, stride=64), :] = back[:N_DP]
            sc_ref[pl.ds(kh * 32 + QL + ql, N_DP, stride=64), :] = back[N_DP:]
    for n in range(N_DP):
        out_ref[n] = sc_ref[n * 64 : (n + 1) * 64, :].astype(bf16)


def weight_kernel(modes_ref, out_ref, x_ref, y_ref):
    for n in range(N_DP):
        x_ref[n * 64 : (n + 1) * 64, :] = modes_ref[n, 0:64, :].astype(f32)
        y_ref[n * 64 : (n + 1) * 64, :] = modes_ref[n, 64:128, :].astype(f32)
    for kh in range(2):
        for ql in range(QL):
            rhs = paired(*load_modes(y_ref, kh, ql))
            lhs = jnp.concatenate(load_modes(x_ref, kh, ql), axis=0).astype(bf16)
            grad = dot(lhs, rhs, TN)
            for kl in range(2):
                mine = grad[kl * C : (kl + 1) * C]
                re = mine[:, kl * C : (kl + 1) * C]
                im = mine[:, 128 + kl * C : 128 + (kl + 1) * C]
                out_ref[ql, kh * 2 + kl] = jnp.concatenate([re, im], axis=1).astype(bf16)


def synth_kernel(modes_ref, m_ref, out_ref, d_ref, sc_ref):
    for q in range(N_DP):
        for kh in range(2):
            d_ref[q * 32 : (q + 1) * 32, kh * 128 : (kh + 1) * 128] = modes_ref[q, kh * 32 : (kh + 1) * 32, :]
    lat = dot(m_ref[...], d_ref[...], TN)
    for part in range(2):
        for l in range(ROWS_DEV):
            at = (part * ROWS_DEV + l) * N_DOMAIN
            for kh in range(2):
                block = lat[at : at + N_DOMAIN, kh * 128 : (kh + 1) * 128]
                sc_ref[l, pl.ds(part * 2 + kh, N_DOMAIN, stride=4), :] = block
    for l in range(ROWS_DEV):
        out_ref[:, :, l * 128 : (l + 1) * 128] = sc_ref[l].reshape(N_DOMAIN, 4, 128).astype(bf16)


def grad_kernel(msg_ref, t_ref, dz_ref, pw_ref, out_hbm, sc_ref, lhs_ref, pd_ref, out_ref, sems):
    for l in range(ROWS_DEV):
        sc_ref[l] = msg_ref[:, :, l * 128 : (l + 1) * 128].astype(f32).reshape(N_DOMAIN * 4, 128)
    pd_ref[...] = jnp.zeros((LC, LC), bf16)
    for l in range(ROWS_DEV):
        blocks = [sc_ref[l, pl.ds(pk, N_DOMAIN, stride=4), :] for pk in range(4)]
        turned = jnp.concatenate(blocks, axis=0).T
        for kl in range(2):
            lhs_ref[l * C : (l + 1) * C, kl * 256 : (kl + 1) * 256] = turned[kl * C : (kl + 1) * C].astype(bf16)
        pd_ref[l * C : (l + 1) * C, l * C : (l + 1) * C] = pw_ref[...]
    step = 384
    copies = []
    for i in range(HALF // step):
        cols = slice(i * step, (i + 1) * step)
        even = dot(lhs_ref[:, :256], t_ref[:256, cols], NN)
        odd = dot(lhs_ref[:, 256:], t_ref[256:, cols], NN)
        for h, spec in enumerate((even + odd, even - odd)):
            cols = slice(h * HALF + i * step, h * HALF + (i + 1) * step)
            out_ref[:, cols] = (spec + dot(pd_ref[...], dz_ref[:, cols], NN)).astype(bf16)
            copies.append(pltpu.make_async_copy(out_ref.at[:, cols], out_hbm.at[:, cols], sems.at[2 * i + h]))
            copies[-1].start()
    for copy in copies:
        copy.wait()


WHOLE = pl.BlockSpec(memory_space=pltpu.VMEM)
FAR = pl.BlockSpec(memory_space=pltpu.HBM)


def call(kernel, outs, scratch, flops, *args, specs=None, out_specs=None, vmem=40):
    nbytes = sum(a.size * a.dtype.itemsize for a in args)
    return pl.pallas_call(
        kernel,
        out_shape=outs,
        in_specs=specs or [WHOLE] * len(args),
        out_specs=jax.tree.map(lambda _: WHOLE, outs) if out_specs is None else out_specs,
        scratch_shapes=scratch,
        cost_estimate=pl.CostEstimate(flops=flops, bytes_accessed=nbytes, transcendentals=0),
        compiler_params=pltpu.CompilerParams(vmem_limit_bytes=vmem * 1024 * 1024),
    )(*args)


def slots_call(inputs, preact, table, readout, observed, cell_index, drift_steps, counts):
    small = [pltpu.VMEM((1, SLOTS), jnp.int32), pltpu.VMEM((1, SLOTS), jnp.int32)]
    return call(
        slots_kernel,
        (
            jax.ShapeDtypeStruct((N_DOMAIN, 8, 384), bf16),
            jax.ShapeDtypeStruct((C, SLOTS), f32),
        ),
        [
            pltpu.VMEM((N_DOMAIN, 8, 384), bf16),
            pltpu.VMEM((C, SLOTS), f32),
            pltpu.VMEM((HALF, SLOTS), bf16),
            pltpu.VMEM((ROWS_DEV, 512, 128), f32),
            pltpu.VMEM((LC, NX), bf16),
            pltpu.VMEM((2 * LC, HALF), bf16),
            pltpu.VMEM((512, HALF), bf16),
            pltpu.VMEM((STEPS, 2, C), f32),
            pltpu.VMEM((2, SLOTS), f32),
            *small,
            pltpu.SemaphoreType.DMA((8,)),
            pltpu.SemaphoreType.DMA((4,)),
        ],
        2 * LC * NX * 512 * 4,
        inputs.reshape(LC, NX),
        preact.reshape(LC, NX),
        table,
        readout,
        observed.reshape(2, SLOTS),
        cell_index,
        drift_steps,
        counts,
        specs=[FAR] * 7 + [pl.BlockSpec(memory_space=pltpu.SMEM)],
        out_specs=(FAR, FAR),
        vmem=59,
    )


def local(inputs, preact, spectral_weight, point_weight, readout, observed, cell_index, drift_steps, counts):
    table = jnp.asarray(lon_table())
    lat = jnp.asarray(lat_table())
    msg, dslot = slots_call(inputs, preact, table, readout, observed, cell_index, drift_steps, counts)
    msg = lax.all_to_all(msg, "domain", 0, 0, tiled=True)
    modes, weight, lat = call(
        lat_kernel,
        (
            jax.ShapeDtypeStruct((N_DP, 128, 128), bf16),
            jax.ShapeDtypeStruct((QL, 4, C, 2 * C), bf16),
            jax.ShapeDtypeStruct(lat.shape, bf16),
        ),
        [pltpu.VMEM((ROWS_DEV, 512, 128), f32), pltpu.VMEM((384, 512), bf16)],
        2 * 256 * 384 * 512,
        msg,
        lat,
        spectral_weight,
    )
    modes = lax.all_to_all(modes, "dp", 0, 0, tiled=True)
    dmodes, lat = call(
        mix_kernel,
        (jax.ShapeDtypeStruct((N_DP, 64, 128), bf16), jax.ShapeDtypeStruct(lat.shape, bf16)),
        [pltpu.VMEM((512, 128), f32), pltpu.VMEM((512, 128), f32)],
        2 * 32 * 128 * 128 * 256,
        modes,
        weight,
        lat,
    )
    dmodes = lax.all_to_all(dmodes, "dp", 0, 0, tiled=True)
    weight_grad = call(
        weight_kernel,
        jax.ShapeDtypeStruct((QL, 4, C, 2 * C), bf16),
        [pltpu.VMEM((512, 128), f32), pltpu.VMEM((512, 128), f32)],
        2 * 32 * 128 * 128 * 256,
        modes,
    )
    dz = call(
        scatter_kernel,
        jax.ShapeDtypeStruct((LC, NX), bf16),
        [pltpu.VMEM((NX, SLOTS), bf16)],
        2 * LC * NX * 512 * 2,
        dslot,
        cell_index,
    )
    msg = call(
        synth_kernel,
        jax.ShapeDtypeStruct((N_DOMAIN, 4, 384), bf16),
        [
            pltpu.VMEM((256, 256), bf16),
            pltpu.VMEM((ROWS_DEV, 256, 128), f32),
        ],
        2 * 256 * 384 * 256,
        dmodes,
        lat,
    )
    msg = lax.all_to_all(msg, "domain", 0, 0, tiled=True)
    input_grad = call(
        grad_kernel,
        jax.ShapeDtypeStruct((LC, NX), bf16),
        [
            pltpu.VMEM((ROWS_DEV, 256, 128), f32),
            pltpu.VMEM((LC, 512), bf16),
            pltpu.VMEM((LC, LC), bf16),
            pltpu.VMEM((LC, NX), bf16),
            pltpu.SemaphoreType.DMA((6,)),
        ],
        2 * LC * NX * 448,
        msg,
        table,
        dz,
        point_weight,
        out_specs=FAR,
    )
    return (input_grad.reshape(1, ROWS_DEV, C, NX), weight_grad)


def solution(mesh):
    placed = (
        P("dp", "domain", None, None),
        P("dp", "domain", None, None),
        P("dp", "domain", None, None),
        P(),
        P(),
        P("dp", None, "domain"),
        P("dp", "domain"),
        P("dp", "domain"),
        P("dp", "domain"),
    )
    return jax.shard_map(
        local,
        mesh=mesh,
        in_specs=placed,
        out_specs=(P("dp", "domain", None, None), P("dp", "domain", None, None)),
        check_vma=False,
    )
```

```python
import numpy as np
import ml_dtypes
import jax
import jax.numpy as jnp
from jax import lax
from jax.experimental import pallas as pl
from jax.experimental.pallas import tpu as pltpu
from jax.sharding import PartitionSpec as P

NX = 2304
NY = 2160
KX = 256
KY = 128
STEPS = 48
SLOTS = 512
C = 64
ROWS_DEV = 3
N_DOMAIN = 64
N_DP = 8
ROWS = ROWS_DEV * N_DOMAIN
QL = KY // N_DP
LC = ROWS_DEV * C
HALF = NX // 2

two_pi = 6.283185307179586
loss_scale = 8.0
gelu_a = 0.7978845608
gelu_b = 0.044715

f32 = jnp.float32
bf16 = jnp.bfloat16


def lon_table():
    kl, part, kh, block = np.meshgrid(np.arange(2), np.arange(2), np.arange(2), np.arange(N_DOMAIN), indexing="ij")
    wavenum = (4 * block + 2 * kh + kl).reshape(-1, 1).astype(np.int64)
    part = part.reshape(-1, 1)
    phase = (wavenum * np.arange(HALF)[None, :] % NX) * (two_pi / NX)
    return np.where(part == 0, np.cos(phase), -np.sin(phase)).astype(ml_dtypes.bfloat16)


def lat_table():
    block, part, ql = np.meshgrid(np.arange(N_DP), np.arange(2), np.arange(QL), indexing="ij")
    part2, l, slab = np.meshgrid(np.arange(2), np.arange(ROWS_DEV), np.arange(N_DOMAIN), indexing="ij")
    index_q = (block * QL + ql).reshape(-1, 1)
    wavenum = np.where(index_q < KY // 2, index_q, NY - KY + index_q).astype(np.int64)
    rows_y = (slab * ROWS_DEV + l).reshape(1, -1) * (NY // ROWS)
    phase = (wavenum * rows_y % NY) * (two_pi / NY)
    part, part2 = part.reshape(-1, 1), part2.reshape(1, -1)
    sine = np.where(part < part2, np.sin(phase), -np.sin(phase))
    return np.where(part == part2, np.cos(phase), sine).astype(ml_dtypes.bfloat16)


def dot(a, b, contract, precision=None):
    return lax.dot_general(a, b, ((contract[0], contract[1]), ((), ())), precision=precision, preferred_element_type=f32)


NN = ((1,), (0,))
NT = ((1,), (1,))
TN = ((0,), (0,))


def where_slots(cell_ref):
    cell = cell_ref[...]
    row = (cell >= NX).astype(jnp.int32) + (cell >= 2 * NX).astype(jnp.int32)
    return row, cell - row * NX


def hot_slots(col, oh_ref):
    step = 128
    for i in range(oh_ref.shape[0] // step):
        here = lax.broadcasted_iota(jnp.int32, (step, SLOTS), 0) + i * step
        oh_ref[i * step : (i + 1) * step, :] = (here == col).astype(f32).astype(bf16)


def spread_slots(row, dslot):
    hi = dslot.astype(bf16).astype(f32)
    lo = dslot - hi
    zero = jnp.zeros((C, SLOTS), f32)
    return [
        jnp.concatenate([jnp.where(row == l, part, zero).astype(bf16) for l in range(ROWS_DEV)], axis=0)
        for part in (hi, lo)
    ]


def slots_kernel(
    x_hbm, p_hbm, t_hbm, ro_hbm, obs_hbm, cell_hbm, step_hbm, cnt_ref, msg_ref, dslot_ref, oh_ref, sc_ref, x_ref, p_ref, t_ref, ro_ref, obs_ref, cell_ref, step_ref, sems,
):
    moves = (
        (cell_hbm, cell_ref),
        (step_hbm, step_ref),
        (obs_hbm, obs_ref),
        (ro_hbm, ro_ref),
        (p_hbm.at[:, :HALF], p_ref.at[:LC]),
        (p_hbm.at[:, HALF:], p_ref.at[LC:]),
        (t_hbm, t_ref),
        (x_hbm, x_ref),
    )
    copies = [pltpu.make_async_copy(src, dst, sems.at[i]) for i, (src, dst) in enumerate(moves)]
    for copy in copies:
        copy.start()
    copies[0].wait()
    row, col = where_slots(cell_ref)
    east = (col >= HALF).astype(jnp.int32)
    hot_slots(col - east * HALF, oh_ref)
    place = east * ROWS_DEV + row
    for copy in copies[1:4]:
        copy.wait()
    step_hot = (lax.broadcasted_iota(jnp.int32, (STEPS, SLOTS), 0) == step_ref[...]).astype(f32).astype(bf16)
    step_hot = jnp.concatenate([step_hot] * 3, axis=0)
    chosen = []
    for j in range(2):
        full = ro_ref[:, j, :]
        top = full.astype(bf16)
        mid = (full - top.astype(f32)).astype(bf16)
        low = (full - top.astype(f32) - mid.astype(f32)).astype(bf16)
        chosen.append(dot(jnp.concatenate([top, mid, low], axis=0), step_hot, TN))
    for copy in copies[4:6]:
        copy.wait()
    zall = dot(p_ref[...], oh_ref[...], NN)
    z = jnp.zeros((C, SLOTS), f32)
    for i in range(2 * ROWS_DEV):
        z = z + jnp.where(place == i, zall[i * C : (i + 1) * C], 0.0)
    copies[6].wait()
    west = dot(t_ref[:256], oh_ref[...], NN).astype(bf16)
    turn = (1 - 2 * east).astype(f32)
    rest = (dot(t_ref[256:], oh_ref[...], NN) * turn).astype(bf16)
    th = jnp.tanh(gelu_a * (z + gelu_b * (z * z * z)))
    act = 0.5 * z * (1.0 + th)
    slope = 0.5 * (1.0 + th) + 0.5 * z * (1.0 - th * th) * (gelu_a * (1.0 + 3.0 * gelu_b * (z * z)))
    live = (lax.broadcasted_iota(jnp.int32, (1, SLOTS), 1) < cnt_ref[0, 0]).astype(f32)
    back = jnp.zeros((C, SLOTS), f32)
    for j in range(2):
        cj = chosen[j]
        velocity = jnp.sum(cj * act, axis=0, keepdims=True)
        back = back + cj * (loss_scale * live * (velocity - obs_ref[j : j + 1, :]))
    dslot = slope * back
    dslot_ref[...] = dslot

    def place_spectra(xz, even, odd):
        for l in range(ROWS_DEV):
            for pk in range(4):
                block = jnp.concatenate(
                    [spec[pk * 64 : (pk + 1) * 64, l * C : (l + 1) * C] for spec in (even, odd)], axis=1
                )
                sc_ref[l, pl.ds(xz * 4 + pk, N_DOMAIN, stride=8), :] = block

    copies[7].wait()
    near, far = x_ref[:, :HALF].astype(f32), x_ref[:, HALF:].astype(f32)
    place_spectra(
        0, dot(t_ref[:256], (near + far).astype(bf16), NT), dot(t_ref[256:], (near - far).astype(bf16), NT)
    )
    hi, lo = spread_slots(row, dslot)
    both = jnp.concatenate([hi, lo], axis=0)
    parts = [dot(waves, both, NT) for waves in (west, rest)]
    place_spectra(1, *[spec[:, :LC] + spec[:, LC:] for spec in parts])
    for l in range(ROWS_DEV):
        msg_ref[:, :, l * 128 : (l + 1) * 128] = sc_ref[l].reshape(N_DOMAIN, 8, 128).astype(bf16)


def scatter_kernel(dslot_ref, cell_ref, dz_ref, oh_ref):
    row, col = where_slots(cell_ref)
    hot_slots(col, oh_ref)
    both = jnp.concatenate(spread_slots(row, dslot_ref[...]), axis=0)
    step = 768
    for i in range(NX // step):
        grid = dot(both, oh_ref[i * step : (i + 1) * step, :], NT)
        dz_ref[:, i * step : (i + 1) * step] = (grid[:LC] + grid[LC:]).astype(bf16)


def lat_kernel(msg_ref, m_ref, w_ref, out_ref, sc_ref, rhs_ref):
    del w_ref
    for l in range(ROWS_DEV):
        sc_ref[l] = msg_ref[:, :, l * 128 : (l + 1) * 128].astype(f32).reshape(N_DOMAIN * 8, 128)
    for xz in range(2):
        for part in range(2):
            for kh in range(2):
                for l in range(ROWS_DEV):
                    block = sc_ref[l, pl.ds(xz * 4 + part * 2 + kh, N_DOMAIN, stride=8), :]
                    at, lane = (part * ROWS_DEV + l) * N_DOMAIN, (xz * 2 + kh) * 128
                    rhs_ref[at : at + N_DOMAIN, lane : lane + 128] = block.astype(bf16)
    lead = (lax.axis_index("domain") == 0) & (lax.broadcasted_iota(jnp.int32, (1, 256), 1) < C)
    scale = jnp.where(lead, 1.0 / (NX * ROWS), 2.0 / (NX * ROWS))
    modes = dot(m_ref[...], rhs_ref[...], NN)
    for xz in range(2):
        for kh in range(2):
            b = xz * 2 + kh
            part = modes[:, b * 128 : (b + 1) * 128]
            if xz == 1:
                part = part * scale[:, kh * 128 : (kh + 1) * 128]
            part = part.astype(bf16)
            for d in range(N_DP):
                out_ref[d, b * 32 : (b + 1) * 32, :] = part[d * 32 : (d + 1) * 32]


def load_modes(ref, kh, ql):
    re = ref[pl.ds(kh * 32 + ql, N_DP, stride=64), :]
    im = ref[pl.ds(kh * 32 + QL + ql, N_DP, stride=64), :]
    return re, im


def paired(re, im):
    top = jnp.concatenate([re, im], axis=1)
    low = jnp.concatenate([im, -re], axis=1)
    return jnp.concatenate([top, low], axis=0).astype(bf16)


def mix_kernel(modes_ref, w_ref, m_ref, out_ref, m_out_ref, y_ref, sc_ref):
    m_out_ref[...] = m_ref[...]
    for n in range(N_DP):
        y_ref[n * 64 : (n + 1) * 64, :] = modes_ref[n, 64:128, :].astype(f32)
    zero = jnp.zeros((C, C), bf16)
    for kh in range(2):
        for ql in range(QL):
            lhs = paired(*load_modes(y_ref, kh, ql))
            w0, w1 = w_ref[ql, kh * 2], w_ref[ql, kh * 2 + 1]
            rhs = jnp.concatenate(
                [
                    jnp.concatenate([w0[:, :C], zero, w0[:, C:], zero], axis=1),
                    jnp.concatenate([zero, w1[:, :C], zero, w1[:, C:]], axis=1),
                ],
                axis=0,
            )
            back = dot(lhs, rhs, NT)
            sc_ref[pl.ds(kh * 32 + ql, N_DP, stride=64), :] = back[:N_DP]
            sc_ref[pl.ds(kh * 32 + QL + ql, N_DP, stride=64), :] = back[N_DP:]
    for n in range(N_DP):
        out_ref[n] = sc_ref[n * 64 : (n + 1) * 64, :].astype(bf16)


def weight_kernel(modes_ref, out_ref, x_ref, y_ref):
    for n in range(N_DP):
        x_ref[n * 64 : (n + 1) * 64, :] = modes_ref[n, 0:64, :].astype(f32)
        y_ref[n * 64 : (n + 1) * 64, :] = modes_ref[n, 64:128, :].astype(f32)
    for kh in range(2):
        for ql in range(QL):
            rhs = paired(*load_modes(y_ref, kh, ql))
            lhs = jnp.concatenate(load_modes(x_ref, kh, ql), axis=0).astype(bf16)
            grad = dot(lhs, rhs, TN)
            for kl in range(2):
                mine = grad[kl * C : (kl + 1) * C]
                re = mine[:, kl * C : (kl + 1) * C]
                im = mine[:, 128 + kl * C : 128 + (kl + 1) * C]
                out_ref[ql, kh * 2 + kl] = jnp.concatenate([re, im], axis=1).astype(bf16)


def synth_kernel(modes_ref, m_ref, out_ref, d_ref, sc_ref):
    for q in range(N_DP):
        for kh in range(2):
            d_ref[q * 32 : (q + 1) * 32, kh * 128 : (kh + 1) * 128] = modes_ref[q, kh * 32 : (kh + 1) * 32, :]
    lat = dot(m_ref[...], d_ref[...], TN)
    for part in range(2):
        for l in range(ROWS_DEV):
            at = (part * ROWS_DEV + l) * N_DOMAIN
            for kh in range(2):
                block = lat[at : at + N_DOMAIN, kh * 128 : (kh + 1) * 128]
                sc_ref[l, pl.ds(part * 2 + kh, N_DOMAIN, stride=4), :] = block
    for l in range(ROWS_DEV):
        out_ref[:, :, l * 128 : (l + 1) * 128] = sc_ref[l].reshape(N_DOMAIN, 4, 128).astype(bf16)


def grad_kernel(msg_ref, t_ref, dz_ref, pw_ref, out_hbm, sc_ref, lhs_ref, pd_ref, out_ref, sems):
    for l in range(ROWS_DEV):
        sc_ref[l] = msg_ref[:, :, l * 128 : (l + 1) * 128].astype(f32).reshape(N_DOMAIN * 4, 128)
    pd_ref[...] = jnp.zeros((LC, LC), bf16)
    for l in range(ROWS_DEV):
        blocks = [sc_ref[l, pl.ds(pk, N_DOMAIN, stride=4), :] for pk in range(4)]
        turned = jnp.concatenate(blocks, axis=0).T
        for kl in range(2):
            lhs_ref[l * C : (l + 1) * C, kl * 256 : (kl + 1) * 256] = turned[kl * C : (kl + 1) * C].astype(bf16)
        pd_ref[l * C : (l + 1) * C, l * C : (l + 1) * C] = pw_ref[...]
    step = 384
    copies = []
    for i in range(HALF // step):
        cols = slice(i * step, (i + 1) * step)
        even = dot(lhs_ref[:, :256], t_ref[:256, cols], NN)
        odd = dot(lhs_ref[:, 256:], t_ref[256:, cols], NN)
        for h, spec in enumerate((even + odd, even - odd)):
            cols = slice(h * HALF + i * step, h * HALF + (i + 1) * step)
            out_ref[:, cols] = (spec + dot(pd_ref[...], dz_ref[:, cols], NN)).astype(bf16)
            copies.append(pltpu.make_async_copy(out_ref.at[:, cols], out_hbm.at[:, cols], sems.at[2 * i + h]))
            copies[-1].start()
    for copy in copies:
        copy.wait()


WHOLE = pl.BlockSpec(memory_space=pltpu.VMEM)
FAR = pl.BlockSpec(memory_space=pltpu.HBM)


def call(kernel, outs, scratch, flops, *args, specs=None, out_specs=None, vmem=40):
    nbytes = sum(a.size * a.dtype.itemsize for a in args)
    return pl.pallas_call(
        kernel,
        out_shape=outs,
        in_specs=specs or [WHOLE] * len(args),
        out_specs=jax.tree.map(lambda _: WHOLE, outs) if out_specs is None else out_specs,
        scratch_shapes=scratch,
        cost_estimate=pl.CostEstimate(flops=flops, bytes_accessed=nbytes, transcendentals=0),
        compiler_params=pltpu.CompilerParams(vmem_limit_bytes=vmem * 1024 * 1024),
    )(*args)


def slots_call(inputs, preact, table, readout, observed, cell_index, drift_steps, counts):
    small = [pltpu.VMEM((1, SLOTS), jnp.int32), pltpu.VMEM((1, SLOTS), jnp.int32)]
    return call(
        slots_kernel,
        (
            jax.ShapeDtypeStruct((N_DOMAIN, 8, 384), bf16),
            jax.ShapeDtypeStruct((C, SLOTS), f32),
        ),
        [
            pltpu.VMEM((HALF, SLOTS), bf16),
            pltpu.VMEM((ROWS_DEV, 512, 128), f32),
            pltpu.VMEM((LC, NX), bf16),
            pltpu.VMEM((2 * LC, HALF), bf16),
            pltpu.VMEM((512, HALF), bf16),
            pltpu.VMEM((STEPS, 2, C), f32),
            pltpu.VMEM((2, SLOTS), f32),
            *small,
            pltpu.SemaphoreType.DMA((8,)),
        ],
        2 * LC * NX * 512 * 4,
        *[
            pltpu.with_memory_space_constraint(array, pltpu.HBM)
            for array in (
                inputs.reshape(LC, NX),
                preact.reshape(LC, NX),
                table,
                readout,
                observed.reshape(2, SLOTS),
                cell_index,
                drift_steps,
            )
        ],
        counts,
        specs=[FAR] * 7 + [pl.BlockSpec(memory_space=pltpu.SMEM)],
    )


def local(inputs, preact, spectral_weight, point_weight, readout, observed, cell_index, drift_steps, counts):
    table = jnp.asarray(lon_table())
    lat = jnp.asarray(lat_table())
    msg, dslot = slots_call(inputs, preact, table, readout, observed, cell_index, drift_steps, counts)
    msg = lax.all_to_all(msg, "domain", 0, 0, tiled=True)
    modes = call(
        lat_kernel,
        jax.ShapeDtypeStruct((N_DP, 128, 128), bf16),
        [pltpu.VMEM((ROWS_DEV, 512, 128), f32), pltpu.VMEM((384, 512), bf16)],
        2 * 256 * 384 * 512,
        msg,
        lat,
        spectral_weight,
    )
    modes = lax.all_to_all(modes, "dp", 0, 0, tiled=True)
    dmodes, lat = call(
        mix_kernel,
        (jax.ShapeDtypeStruct((N_DP, 64, 128), bf16), jax.ShapeDtypeStruct(lat.shape, bf16)),
        [pltpu.VMEM((512, 128), f32), pltpu.VMEM((512, 128), f32)],
        2 * 32 * 128 * 128 * 256,
        modes,
        spectral_weight,
        lat,
    )
    dmodes = lax.all_to_all(dmodes, "dp", 0, 0, tiled=True)
    weight_grad = call(
        weight_kernel,
        jax.ShapeDtypeStruct((QL, 4, C, 2 * C), bf16),
        [pltpu.VMEM((512, 128), f32), pltpu.VMEM((512, 128), f32)],
        2 * 32 * 128 * 128 * 256,
        modes,
    )
    dz = call(
        scatter_kernel,
        jax.ShapeDtypeStruct((LC, NX), bf16),
        [pltpu.VMEM((NX, SLOTS), bf16)],
        2 * LC * NX * 512 * 2,
        dslot,
        cell_index,
    )
    msg = call(
        synth_kernel,
        jax.ShapeDtypeStruct((N_DOMAIN, 4, 384), bf16),
        [
            pltpu.VMEM((256, 256), bf16),
            pltpu.VMEM((ROWS_DEV, 256, 128), f32),
        ],
        2 * 256 * 384 * 256,
        dmodes,
        lat,
    )
    msg = lax.all_to_all(msg, "domain", 0, 0, tiled=True)
    input_grad = call(
        grad_kernel,
        jax.ShapeDtypeStruct((LC, NX), bf16),
        [
            pltpu.VMEM((ROWS_DEV, 256, 128), f32),
            pltpu.VMEM((LC, 512), bf16),
            pltpu.VMEM((LC, LC), bf16),
            pltpu.VMEM((LC, NX), bf16),
            pltpu.SemaphoreType.DMA((6,)),
        ],
        2 * LC * NX * 448,
        msg,
        table,
        dz,
        point_weight,
        out_specs=FAR,
    )
    return (input_grad.reshape(1, ROWS_DEV, C, NX), weight_grad)


def solution(mesh):
    placed = (
        P("dp", "domain", None, None),
        P("dp", "domain", None, None),
        P("dp", "domain", None, None),
        P(),
        P(),
        P("dp", None, "domain"),
        P("dp", "domain"),
        P("dp", "domain"),
        P("dp", "domain"),
    )
    return jax.shard_map(
        local,
        mesh=mesh,
        in_specs=placed,
        out_specs=(P("dp", "domain", None, None), P("dp", "domain", None, None)),
        check_vma=False,
    )
```

```python
import numpy as np
import ml_dtypes
import jax
import jax.numpy as jnp
from jax import lax
from jax.experimental import pallas as pl
from jax.experimental.pallas import tpu as pltpu
from jax.sharding import PartitionSpec as P

NX = 2304
NY = 2160
KX = 256
KY = 128
STEPS = 48
SLOTS = 512
C = 64
ROWS_DEV = 3
N_DOMAIN = 64
N_DP = 8
ROWS = ROWS_DEV * N_DOMAIN
QL = KY // N_DP
LC = ROWS_DEV * C
HALF = NX // 2
EDGES = (0, 640, 1152)

two_pi = 6.283185307179586
loss_scale = 8.0
gelu_a = 0.7978845608
gelu_b = 0.044715

f32 = jnp.float32
bf16 = jnp.bfloat16


def lon_table():
    kl, part, kh, block = np.meshgrid(np.arange(2), np.arange(2), np.arange(2), np.arange(N_DOMAIN), indexing="ij")
    wavenum = (4 * block + 2 * kh + kl).reshape(-1, 1).astype(np.int64)
    part = part.reshape(-1, 1)
    phase = (wavenum * np.arange(HALF)[None, :] % NX) * (two_pi / NX)
    return np.where(part == 0, np.cos(phase), -np.sin(phase)).astype(ml_dtypes.bfloat16)


def lat_table():
    block, part, ql = np.meshgrid(np.arange(N_DP), np.arange(2), np.arange(QL), indexing="ij")
    part2, l, slab = np.meshgrid(np.arange(2), np.arange(ROWS_DEV), np.arange(N_DOMAIN), indexing="ij")
    index_q = (block * QL + ql).reshape(-1, 1)
    wavenum = np.where(index_q < KY // 2, index_q, NY - KY + index_q).astype(np.int64)
    rows_y = (slab * ROWS_DEV + l).reshape(1, -1) * (NY // ROWS)
    phase = (wavenum * rows_y % NY) * (two_pi / NY)
    part, part2 = part.reshape(-1, 1), part2.reshape(1, -1)
    sine = np.where(part < part2, np.sin(phase), -np.sin(phase))
    return np.where(part == part2, np.cos(phase), sine).astype(ml_dtypes.bfloat16)


def dot(a, b, contract, precision=None):
    return lax.dot_general(a, b, ((contract[0], contract[1]), ((), ())), precision=precision, preferred_element_type=f32)


NN = ((1,), (0,))
NT = ((1,), (1,))
TN = ((0,), (0,))


def where_slots(cell_ref):
    cell = cell_ref[...]
    row = (cell >= NX).astype(jnp.int32) + (cell >= 2 * NX).astype(jnp.int32)
    return row, cell - row * NX


def hot_slots(col, oh_ref):
    step = 128
    for i in range(oh_ref.shape[0] // step):
        here = lax.broadcasted_iota(jnp.int32, (step, SLOTS), 0) + i * step
        oh_ref[i * step : (i + 1) * step, :] = (here == col).astype(f32).astype(bf16)


def turn(steps):
    steps = steps - NX * jnp.floor(steps * (1.0 / NX) + 0.5)
    quarter = jnp.floor(steps * (4.0 / NX) + 0.5)
    a = (steps - (NX // 4) * quarter) * (two_pi / NX)
    b = a * a
    cosine = 1.0 + b * (-1 / 2 + b * (1 / 24 + b * (-1 / 720 + b * (1 / 40320))))
    sine = a * (1.0 + b * (-1 / 6 + b * (1 / 120 + b * (-1 / 5040 + b * (1 / 362880)))))
    odd = jnp.abs(quarter) == 1.0
    cosine, sine = jnp.where(odd, sine, cosine), jnp.where(odd, cosine, sine)
    cosine = jnp.where((quarter == 1.0) | (jnp.abs(quarter) == 2.0), -cosine, cosine)
    return cosine, jnp.where((quarter < 0.0) | (quarter == 2.0), -sine, sine)


def slot_waves(col, out_ref):
    x = col.astype(f32)
    block = lax.broadcasted_iota(jnp.int32, (N_DOMAIN, SLOTS), 0).astype(f32)
    cos4, sin4 = turn(4.0 * block * x)
    for kl in range(2):
        for kh in range(2):
            cosj, sinj = turn((2.0 * kh + kl) * x)
            at = kl * 256 + kh * 64
            out_ref[at : at + 64, :] = (cos4 * cosj - sin4 * sinj).astype(bf16)
            out_ref[at + 128 : at + 192, :] = (-sin4 * cosj - cos4 * sinj).astype(bf16)


def spread_slots(row, dslot):
    hi = dslot.astype(bf16).astype(f32)
    lo = dslot - hi
    zero = jnp.zeros((C, SLOTS), f32)
    return [
        jnp.concatenate([jnp.where(row == l, part, zero).astype(bf16) for l in range(ROWS_DEV)], axis=0)
        for part in (hi, lo)
    ]


def slots_kernel(
    x_hbm, p_hbm, t_hbm, ro_hbm, obs_hbm, cell_hbm, step_hbm, cnt_ref, msg_ref, dslot_ref, oh_ref, wave_ref, sc_ref, x_ref, p_ref, t_ref, ro_ref, obs_ref, cell_ref, step_ref, sems,
):
    moves = (
        (cell_hbm, cell_ref),
        (step_hbm, step_ref),
        (obs_hbm, obs_ref),
        (ro_hbm, ro_ref),
        (p_hbm.at[:, :HALF], p_ref.at[:LC]),
        (p_hbm.at[:, HALF:], p_ref.at[LC:]),
        (t_hbm, t_ref),
        (x_hbm, x_ref),
    )
    copies = [pltpu.make_async_copy(src, dst, sems.at[i]) for i, (src, dst) in enumerate(moves)]
    for copy in copies:
        copy.start()
    copies[0].wait()
    row, col = where_slots(cell_ref)
    east = (col >= HALF).astype(jnp.int32)
    hot_slots(col - east * HALF, oh_ref)
    slot_waves(col, wave_ref)
    place = east * ROWS_DEV + row
    for copy in copies[1:4]:
        copy.wait()
    step_hot = (lax.broadcasted_iota(jnp.int32, (STEPS, SLOTS), 0) == step_ref[...]).astype(f32).astype(bf16)
    step_hot = jnp.concatenate([step_hot] * 3, axis=0)
    chosen = []
    for j in range(2):
        full = ro_ref[:, j, :]
        top = full.astype(bf16)
        mid = (full - top.astype(f32)).astype(bf16)
        low = (full - top.astype(f32) - mid.astype(f32)).astype(bf16)
        chosen.append(dot(jnp.concatenate([top, mid, low], axis=0), step_hot, TN))
    for copy in copies[4:6]:
        copy.wait()
    zall = dot(p_ref[...], oh_ref[...], NN)
    z = jnp.zeros((C, SLOTS), f32)
    for i in range(2 * ROWS_DEV):
        z = z + jnp.where(place == i, zall[i * C : (i + 1) * C], 0.0)
    th = jnp.tanh(gelu_a * (z + gelu_b * (z * z * z)))
    act = 0.5 * z * (1.0 + th)
    slope = 0.5 * (1.0 + th) + 0.5 * z * (1.0 - th * th) * (gelu_a * (1.0 + 3.0 * gelu_b * (z * z)))
    live = (lax.broadcasted_iota(jnp.int32, (1, SLOTS), 1) < cnt_ref[0, 0]).astype(f32)
    back = jnp.zeros((C, SLOTS), f32)
    for j in range(2):
        cj = chosen[j]
        velocity = jnp.sum(cj * act, axis=0, keepdims=True)
        back = back + cj * (loss_scale * live * (velocity - obs_ref[j : j + 1, :]))
    dslot = slope * back
    dslot_ref[...] = dslot

    def place_spectra(xz, even, odd):
        for l in range(ROWS_DEV):
            for pk in range(4):
                block = jnp.concatenate(
                    [spec[pk * 64 : (pk + 1) * 64, l * C : (l + 1) * C] for spec in (even, odd)], axis=1
                )
                sc_ref[l, pl.ds(xz * 4 + pk, N_DOMAIN, stride=8), :] = block

    copies[6].wait()
    copies[7].wait()
    near, far = x_ref[:, :HALF].astype(f32), x_ref[:, HALF:].astype(f32)
    place_spectra(
        0, dot(t_ref[:256], (near + far).astype(bf16), NT), dot(t_ref[256:], (near - far).astype(bf16), NT)
    )
    hi, lo = spread_slots(row, dslot)
    both = jnp.concatenate([hi, lo], axis=0)
    parts = [dot(waves, both, NT) for waves in (wave_ref[:256], wave_ref[256:])]
    place_spectra(1, *[spec[:, :LC] + spec[:, LC:] for spec in parts])
    for l in range(ROWS_DEV):
        msg_ref[:, :, l * 128 : (l + 1) * 128] = sc_ref[l].reshape(N_DOMAIN, 8, 128).astype(bf16)


def scatter_kernel(dslot_ref, cell_ref, dz_ref, oh_ref):
    row, col = where_slots(cell_ref)
    hot_slots(col, oh_ref)
    both = jnp.concatenate(spread_slots(row, dslot_ref[...]), axis=0)
    step = 768
    for i in range(NX // step):
        grid = dot(both, oh_ref[i * step : (i + 1) * step, :], NT)
        dz_ref[:, i * step : (i + 1) * step] = (grid[:LC] + grid[LC:]).astype(bf16)


def lat_kernel(msg_ref, m_ref, w_ref, out_ref, sc_ref, rhs_ref):
    del w_ref
    for l in range(ROWS_DEV):
        sc_ref[l] = msg_ref[:, :, l * 128 : (l + 1) * 128].astype(f32).reshape(N_DOMAIN * 8, 128)
    for xz in range(2):
        for part in range(2):
            for kh in range(2):
                for l in range(ROWS_DEV):
                    block = sc_ref[l, pl.ds(xz * 4 + part * 2 + kh, N_DOMAIN, stride=8), :]
                    at, lane = (part * ROWS_DEV + l) * N_DOMAIN, (xz * 2 + kh) * 128
                    rhs_ref[at : at + N_DOMAIN, lane : lane + 128] = block.astype(bf16)
    lead = (lax.axis_index("domain") == 0) & (lax.broadcasted_iota(jnp.int32, (1, 256), 1) < C)
    scale = jnp.where(lead, 1.0 / (NX * ROWS), 2.0 / (NX * ROWS))
    modes = dot(m_ref[...], rhs_ref[...], NN)
    for xz in range(2):
        for kh in range(2):
            b = xz * 2 + kh
            part = modes[:, b * 128 : (b + 1) * 128]
            if xz == 1:
                part = part * scale[:, kh * 128 : (kh + 1) * 128]
            part = part.astype(bf16)
            for d in range(N_DP):
                out_ref[d, b * 32 : (b + 1) * 32, :] = part[d * 32 : (d + 1) * 32]


def load_modes(ref, kh, ql):
    re = ref[pl.ds(kh * 32 + ql, N_DP, stride=64), :]
    im = ref[pl.ds(kh * 32 + QL + ql, N_DP, stride=64), :]
    return re, im


def paired(re, im):
    top = jnp.concatenate([re, im], axis=1)
    low = jnp.concatenate([im, -re], axis=1)
    return jnp.concatenate([top, low], axis=0).astype(bf16)


def mix_kernel(modes_ref, w_ref, m_ref, out_ref, m_out_ref, y_ref, sc_ref):
    m_out_ref[...] = m_ref[...]
    for n in range(N_DP):
        y_ref[n * 64 : (n + 1) * 64, :] = modes_ref[n, 64:128, :].astype(f32)
    zero = jnp.zeros((C, C), bf16)
    for kh in range(2):
        for ql in range(QL):
            lhs = paired(*load_modes(y_ref, kh, ql))
            w0, w1 = w_ref[ql, kh * 2], w_ref[ql, kh * 2 + 1]
            rhs = jnp.concatenate(
                [
                    jnp.concatenate([w0[:, :C], zero, w0[:, C:], zero], axis=1),
                    jnp.concatenate([zero, w1[:, :C], zero, w1[:, C:]], axis=1),
                ],
                axis=0,
            )
            back = dot(lhs, rhs, NT)
            sc_ref[pl.ds(kh * 32 + ql, N_DP, stride=64), :] = back[:N_DP]
            sc_ref[pl.ds(kh * 32 + QL + ql, N_DP, stride=64), :] = back[N_DP:]
    for n in range(N_DP):
        out_ref[n] = sc_ref[n * 64 : (n + 1) * 64, :].astype(bf16)


def weight_kernel(modes_ref, out_ref, x_ref, y_ref):
    for n in range(N_DP):
        x_ref[n * 64 : (n + 1) * 64, :] = modes_ref[n, 0:64, :].astype(f32)
        y_ref[n * 64 : (n + 1) * 64, :] = modes_ref[n, 64:128, :].astype(f32)
    for kh in range(2):
        for ql in range(QL):
            rhs = paired(*load_modes(y_ref, kh, ql))
            lhs = jnp.concatenate(load_modes(x_ref, kh, ql), axis=0).astype(bf16)
            grad = dot(lhs, rhs, TN)
            for kl in range(2):
                mine = grad[kl * C : (kl + 1) * C]
                re = mine[:, kl * C : (kl + 1) * C]
                im = mine[:, 128 + kl * C : 128 + (kl + 1) * C]
                out_ref[ql, kh * 2 + kl] = jnp.concatenate([re, im], axis=1).astype(bf16)


def synth_kernel(modes_ref, m_ref, out_ref, d_ref, sc_ref):
    for q in range(N_DP):
        for kh in range(2):
            d_ref[q * 32 : (q + 1) * 32, kh * 128 : (kh + 1) * 128] = modes_ref[q, kh * 32 : (kh + 1) * 32, :]
    lat = dot(m_ref[...], d_ref[...], TN)
    for part in range(2):
        for l in range(ROWS_DEV):
            at = (part * ROWS_DEV + l) * N_DOMAIN
            for kh in range(2):
                block = lat[at : at + N_DOMAIN, kh * 128 : (kh + 1) * 128]
                sc_ref[l, pl.ds(part * 2 + kh, N_DOMAIN, stride=4), :] = block
    for l in range(ROWS_DEV):
        out_ref[:, :, l * 128 : (l + 1) * 128] = sc_ref[l].reshape(N_DOMAIN, 4, 128).astype(bf16)


def grad_kernel(msg_ref, t_ref, dz_ref, pw_ref, out_hbm, sc_ref, lhs_ref, pd_ref, out_ref, sems):
    for l in range(ROWS_DEV):
        sc_ref[l] = msg_ref[:, :, l * 128 : (l + 1) * 128].astype(f32).reshape(N_DOMAIN * 4, 128)
    pd_ref[...] = jnp.zeros((LC, LC), bf16)
    for l in range(ROWS_DEV):
        blocks = [sc_ref[l, pl.ds(pk, N_DOMAIN, stride=4), :] for pk in range(4)]
        turned = jnp.concatenate(blocks, axis=0).T
        for kl in range(2):
            lhs_ref[l * C : (l + 1) * C, kl * 256 : (kl + 1) * 256] = turned[kl * C : (kl + 1) * C].astype(bf16)
        pd_ref[l * C : (l + 1) * C, l * C : (l + 1) * C] = pw_ref[...]
    copies = []
    for lo, hi in zip(EDGES[:-1], EDGES[1:]):
        cols = slice(lo, hi)
        even = dot(lhs_ref[:, :256], t_ref[:256, cols], NN)
        odd = dot(lhs_ref[:, 256:], t_ref[256:, cols], NN)
        for h, spec in enumerate((even + odd, even - odd)):
            cols = slice(h * HALF + lo, h * HALF + hi)
            out_ref[:, cols] = (spec + dot(pd_ref[...], dz_ref[:, cols], NN)).astype(bf16)
            copies.append(pltpu.make_async_copy(out_ref.at[:, cols], out_hbm.at[:, cols], sems.at[len(copies)]))
            copies[-1].start()
    for copy in copies:
        copy.wait()


WHOLE = pl.BlockSpec(memory_space=pltpu.VMEM)
FAR = pl.BlockSpec(memory_space=pltpu.HBM)


def call(kernel, outs, scratch, flops, *args, specs=None, out_specs=None, vmem=40):
    nbytes = sum(a.size * a.dtype.itemsize for a in args)
    return pl.pallas_call(
        kernel,
        out_shape=outs,
        in_specs=specs or [WHOLE] * len(args),
        out_specs=jax.tree.map(lambda _: WHOLE, outs) if out_specs is None else out_specs,
        scratch_shapes=scratch,
        cost_estimate=pl.CostEstimate(flops=flops, bytes_accessed=nbytes, transcendentals=0),
        compiler_params=pltpu.CompilerParams(vmem_limit_bytes=vmem * 1024 * 1024),
    )(*args)


def slots_call(inputs, preact, table, readout, observed, cell_index, drift_steps, counts):
    small = [pltpu.VMEM((1, SLOTS), jnp.int32), pltpu.VMEM((1, SLOTS), jnp.int32)]
    return call(
        slots_kernel,
        (
            jax.ShapeDtypeStruct((N_DOMAIN, 8, 384), bf16),
            jax.ShapeDtypeStruct((C, SLOTS), f32),
        ),
        [
            pltpu.VMEM((HALF, SLOTS), bf16),
            pltpu.VMEM((512, SLOTS), bf16),
            pltpu.VMEM((ROWS_DEV, 512, 128), f32),
            pltpu.VMEM((LC, NX), bf16),
            pltpu.VMEM((2 * LC, HALF), bf16),
            pltpu.VMEM((512, HALF), bf16),
            pltpu.VMEM((STEPS, 2, C), f32),
            pltpu.VMEM((2, SLOTS), f32),
            *small,
            pltpu.SemaphoreType.DMA((8,)),
        ],
        2 * LC * NX * 512 * 4,
        *[
            pltpu.with_memory_space_constraint(array, pltpu.HBM)
            for array in (
                inputs.reshape(LC, NX),
                preact.reshape(LC, NX),
                table,
                readout,
                observed.reshape(2, SLOTS),
                cell_index,
                drift_steps,
            )
        ],
        counts,
        specs=[FAR] * 7 + [pl.BlockSpec(memory_space=pltpu.SMEM)],
    )


def grad_call(msg, table, dz, point_weight):
    return call(
        grad_kernel,
        jax.ShapeDtypeStruct((LC, NX), bf16),
        [
            pltpu.VMEM((ROWS_DEV, 256, 128), f32),
            pltpu.VMEM((LC, 512), bf16),
            pltpu.VMEM((LC, LC), bf16),
            pltpu.VMEM((LC, NX), bf16),
            pltpu.SemaphoreType.DMA((2 * len(EDGES),)),
        ],
        2 * LC * NX * 448,
        msg,
        table,
        dz,
        point_weight,
        out_specs=FAR,
    )


def local(inputs, preact, spectral_weight, point_weight, readout, observed, cell_index, drift_steps, counts):
    table = jnp.asarray(lon_table())
    lat = jnp.asarray(lat_table())
    msg, dslot = slots_call(inputs, preact, table, readout, observed, cell_index, drift_steps, counts)
    msg = lax.all_to_all(msg, "domain", 0, 0, tiled=True)
    modes = call(
        lat_kernel,
        jax.ShapeDtypeStruct((N_DP, 128, 128), bf16),
        [pltpu.VMEM((ROWS_DEV, 512, 128), f32), pltpu.VMEM((384, 512), bf16)],
        2 * 256 * 384 * 512,
        msg,
        lat,
        spectral_weight,
    )
    modes = lax.all_to_all(modes, "dp", 0, 0, tiled=True)
    dmodes, lat = call(
        mix_kernel,
        (jax.ShapeDtypeStruct((N_DP, 64, 128), bf16), jax.ShapeDtypeStruct(lat.shape, bf16)),
        [pltpu.VMEM((512, 128), f32), pltpu.VMEM((512, 128), f32)],
        2 * 32 * 128 * 128 * 256,
        modes,
        spectral_weight,
        lat,
    )
    dmodes = lax.all_to_all(dmodes, "dp", 0, 0, tiled=True)
    weight_grad = call(
        weight_kernel,
        jax.ShapeDtypeStruct((QL, 4, C, 2 * C), bf16),
        [pltpu.VMEM((512, 128), f32), pltpu.VMEM((512, 128), f32)],
        2 * 32 * 128 * 128 * 256,
        modes,
    )
    dz = call(
        scatter_kernel,
        jax.ShapeDtypeStruct((LC, NX), bf16),
        [pltpu.VMEM((NX, SLOTS), bf16)],
        2 * LC * NX * 512 * 2,
        dslot,
        cell_index,
    )
    msg = call(
        synth_kernel,
        jax.ShapeDtypeStruct((N_DOMAIN, 4, 384), bf16),
        [
            pltpu.VMEM((256, 256), bf16),
            pltpu.VMEM((ROWS_DEV, 256, 128), f32),
        ],
        2 * 256 * 384 * 256,
        dmodes,
        lat,
    )
    msg = lax.all_to_all(msg, "domain", 0, 0, tiled=True)
    input_grad = grad_call(msg, table, dz, point_weight)
    return (input_grad.reshape(1, ROWS_DEV, C, NX), weight_grad)


def solution(mesh):
    placed = (
        P("dp", "domain", None, None),
        P("dp", "domain", None, None),
        P("dp", "domain", None, None),
        P(),
        P(),
        P("dp", None, "domain"),
        P("dp", "domain"),
        P("dp", "domain"),
        P("dp", "domain"),
    )
    return jax.shard_map(
        local,
        mesh=mesh,
        in_specs=placed,
        out_specs=(P("dp", "domain", None, None), P("dp", "domain", None, None)),
        check_vma=False,
    )
```

```python
import numpy as np
import ml_dtypes
import jax
import jax.numpy as jnp
from jax import lax
from jax.experimental import pallas as pl
from jax.experimental.pallas import tpu as pltpu
from jax.sharding import PartitionSpec as P

NX = 2304
NY = 2160
KX = 256
KY = 128
STEPS = 48
SLOTS = 512
C = 64
ROWS_DEV = 3
N_DOMAIN = 64
N_DP = 8
ROWS = ROWS_DEV * N_DOMAIN
QL = KY // N_DP
LC = ROWS_DEV * C
HALF = NX // 2
EDGES = (0, 640, 1152)

two_pi = 6.283185307179586
loss_scale = 8.0
gelu_a = 0.7978845608
gelu_b = 0.044715

f32 = jnp.float32
bf16 = jnp.bfloat16


def lon_table():
    kl, part, kh, block = np.meshgrid(np.arange(2), np.arange(2), np.arange(2), np.arange(N_DOMAIN), indexing="ij")
    wavenum = (4 * block + 2 * kh + kl).reshape(-1, 1).astype(np.int64)
    part = part.reshape(-1, 1)
    phase = (wavenum * np.arange(HALF)[None, :] % NX) * (two_pi / NX)
    return np.where(part == 0, np.cos(phase), -np.sin(phase)).astype(ml_dtypes.bfloat16)


def lat_table():
    block, part, ql = np.meshgrid(np.arange(N_DP), np.arange(2), np.arange(QL), indexing="ij")
    part2, l, slab = np.meshgrid(np.arange(2), np.arange(ROWS_DEV), np.arange(N_DOMAIN), indexing="ij")
    index_q = (block * QL + ql).reshape(-1, 1)
    wavenum = np.where(index_q < KY // 2, index_q, NY - KY + index_q).astype(np.int64)
    rows_y = (slab * ROWS_DEV + l).reshape(1, -1) * (NY // ROWS)
    phase = (wavenum * rows_y % NY) * (two_pi / NY)
    part, part2 = part.reshape(-1, 1), part2.reshape(1, -1)
    sine = np.where(part < part2, np.sin(phase), -np.sin(phase))
    return np.where(part == part2, np.cos(phase), sine).astype(ml_dtypes.bfloat16)


def dot(a, b, contract, precision=None):
    return lax.dot_general(a, b, ((contract[0], contract[1]), ((), ())), precision=precision, preferred_element_type=f32)


NN = ((1,), (0,))
NT = ((1,), (1,))
TN = ((0,), (0,))


def where_slots(cell_ref):
    cell = cell_ref[...]
    row = (cell >= NX).astype(jnp.int32) + (cell >= 2 * NX).astype(jnp.int32)
    return row, cell - row * NX


def hot_slots(col, oh_ref):
    step = 128
    for i in range(oh_ref.shape[0] // step):
        here = lax.broadcasted_iota(jnp.int32, (step, SLOTS), 0) + i * step
        oh_ref[i * step : (i + 1) * step, :] = (here == col).astype(f32).astype(bf16)


def turn(steps):
    steps = steps - NX * jnp.floor(steps * (1.0 / NX) + 0.5)
    quarter = jnp.floor(steps * (4.0 / NX) + 0.5)
    a = (steps - (NX // 4) * quarter) * (two_pi / NX)
    b = a * a
    cosine = 1.0 + b * (-1 / 2 + b * (1 / 24 + b * (-1 / 720 + b * (1 / 40320))))
    sine = a * (1.0 + b * (-1 / 6 + b * (1 / 120 + b * (-1 / 5040 + b * (1 / 362880)))))
    odd = jnp.abs(quarter) == 1.0
    cosine, sine = jnp.where(odd, sine, cosine), jnp.where(odd, cosine, sine)
    cosine = jnp.where((quarter == 1.0) | (jnp.abs(quarter) == 2.0), -cosine, cosine)
    return cosine, jnp.where((quarter < 0.0) | (quarter == 2.0), -sine, sine)


def slot_waves(col, out_ref):
    x = col.astype(f32)
    block = lax.broadcasted_iota(jnp.int32, (N_DOMAIN, SLOTS), 0).astype(f32)
    cos4, sin4 = turn(4.0 * block * x)
    for kl in range(2):
        for kh in range(2):
            cosj, sinj = turn((2.0 * kh + kl) * x)
            at = kl * 256 + kh * 64
            out_ref[at : at + 64, :] = (cos4 * cosj - sin4 * sinj).astype(bf16)
            out_ref[at + 128 : at + 192, :] = (-sin4 * cosj - cos4 * sinj).astype(bf16)


def spread_slots(row, dslot):
    hi = dslot.astype(bf16).astype(f32)
    lo = dslot - hi
    zero = jnp.zeros((C, SLOTS), f32)
    return [
        jnp.concatenate([jnp.where(row == l, part, zero).astype(bf16) for l in range(ROWS_DEV)], axis=0)
        for part in (hi, lo)
    ]


def slots_kernel(
    x_hbm, p_hbm, t_hbm, ro_hbm, obs_hbm, cell_hbm, step_hbm, w_hbm, m_hbm, cnt_ref, msg_ref, dslot_ref, w_ref, m_ref, oh_ref, wave_ref, sc_ref, x_ref, p_ref, t_ref, ro_ref, obs_ref, cell_ref, step_ref, sems,
):
    moves = (
        (cell_hbm, cell_ref),
        (step_hbm, step_ref),
        (obs_hbm, obs_ref),
        (ro_hbm, ro_ref),
        (p_hbm.at[:, :HALF], p_ref.at[:LC]),
        (p_hbm.at[:, HALF:], p_ref.at[LC:]),
        (t_hbm, t_ref),
        (x_hbm, x_ref),
        (m_hbm, m_ref),
        (w_hbm, w_ref),
    )
    copies = [pltpu.make_async_copy(src, dst, sems.at[i]) for i, (src, dst) in enumerate(moves)]
    for copy in copies:
        copy.start()
    copies[0].wait()
    row, col = where_slots(cell_ref)
    east = (col >= HALF).astype(jnp.int32)
    hot_slots(col - east * HALF, oh_ref)
    slot_waves(col, wave_ref)
    place = east * ROWS_DEV + row
    for copy in copies[1:4]:
        copy.wait()
    step_hot = (lax.broadcasted_iota(jnp.int32, (STEPS, SLOTS), 0) == step_ref[...]).astype(f32).astype(bf16)
    step_hot = jnp.concatenate([step_hot] * 3, axis=0)
    chosen = []
    for j in range(2):
        full = ro_ref[:, j, :]
        top = full.astype(bf16)
        mid = (full - top.astype(f32)).astype(bf16)
        low = (full - top.astype(f32) - mid.astype(f32)).astype(bf16)
        chosen.append(dot(jnp.concatenate([top, mid, low], axis=0), step_hot, TN))
    for copy in copies[4:6]:
        copy.wait()
    zall = dot(p_ref[...], oh_ref[...], NN)
    z = jnp.zeros((C, SLOTS), f32)
    for i in range(2 * ROWS_DEV):
        z = z + jnp.where(place == i, zall[i * C : (i + 1) * C], 0.0)
    th = jnp.tanh(gelu_a * (z + gelu_b * (z * z * z)))
    act = 0.5 * z * (1.0 + th)
    slope = 0.5 * (1.0 + th) + 0.5 * z * (1.0 - th * th) * (gelu_a * (1.0 + 3.0 * gelu_b * (z * z)))
    live = (lax.broadcasted_iota(jnp.int32, (1, SLOTS), 1) < cnt_ref[0, 0]).astype(f32)
    back = jnp.zeros((C, SLOTS), f32)
    for j in range(2):
        cj = chosen[j]
        velocity = jnp.sum(cj * act, axis=0, keepdims=True)
        back = back + cj * (loss_scale * live * (velocity - obs_ref[j : j + 1, :]))
    dslot = slope * back
    dslot_ref[...] = dslot

    def place_spectra(xz, even, odd):
        for l in range(ROWS_DEV):
            for pk in range(4):
                block = jnp.concatenate(
                    [spec[pk * 64 : (pk + 1) * 64, l * C : (l + 1) * C] for spec in (even, odd)], axis=1
                )
                sc_ref[l, pl.ds(xz * 4 + pk, N_DOMAIN, stride=8), :] = block

    copies[6].wait()
    copies[7].wait()
    near, far = x_ref[:, :HALF].astype(f32), x_ref[:, HALF:].astype(f32)
    place_spectra(
        0, dot(t_ref[:256], (near + far).astype(bf16), NT), dot(t_ref[256:], (near - far).astype(bf16), NT)
    )
    hi, lo = spread_slots(row, dslot)
    both = jnp.concatenate([hi, lo], axis=0)
    parts = [dot(waves, both, NT) for waves in (wave_ref[:256], wave_ref[256:])]
    place_spectra(1, *[spec[:, :LC] + spec[:, LC:] for spec in parts])
    for l in range(ROWS_DEV):
        msg_ref[:, :, l * 128 : (l + 1) * 128] = sc_ref[l].reshape(N_DOMAIN, 8, 128).astype(bf16)
    copies[8].wait()
    copies[9].wait()


def scatter_kernel(dslot_ref, cell_ref, dz_ref, oh_ref):
    row, col = where_slots(cell_ref)
    hot_slots(col, oh_ref)
    both = jnp.concatenate(spread_slots(row, dslot_ref[...]), axis=0)
    step = 768
    for i in range(NX // step):
        grid = dot(both, oh_ref[i * step : (i + 1) * step, :], NT)
        dz_ref[:, i * step : (i + 1) * step] = (grid[:LC] + grid[LC:]).astype(bf16)


def lat_kernel(msg_ref, m_ref, out_ref, sc_ref, rhs_ref):
    for l in range(ROWS_DEV):
        sc_ref[l] = msg_ref[:, :, l * 128 : (l + 1) * 128].astype(f32).reshape(N_DOMAIN * 8, 128)
    for xz in range(2):
        for part in range(2):
            for kh in range(2):
                for l in range(ROWS_DEV):
                    block = sc_ref[l, pl.ds(xz * 4 + part * 2 + kh, N_DOMAIN, stride=8), :]
                    at, lane = (part * ROWS_DEV + l) * N_DOMAIN, (xz * 2 + kh) * 128
                    rhs_ref[at : at + N_DOMAIN, lane : lane + 128] = block.astype(bf16)
    lead = (lax.axis_index("domain") == 0) & (lax.broadcasted_iota(jnp.int32, (1, 256), 1) < C)
    scale = jnp.where(lead, 1.0 / (NX * ROWS), 2.0 / (NX * ROWS))
    modes = dot(m_ref[...], rhs_ref[...], NN)
    for xz in range(2):
        for kh in range(2):
            b = xz * 2 + kh
            part = modes[:, b * 128 : (b + 1) * 128]
            if xz == 1:
                part = part * scale[:, kh * 128 : (kh + 1) * 128]
            part = part.astype(bf16)
            for d in range(N_DP):
                out_ref[d, b * 32 : (b + 1) * 32, :] = part[d * 32 : (d + 1) * 32]


def load_modes(ref, kh, ql):
    re = ref[pl.ds(kh * 32 + ql, N_DP, stride=64), :]
    im = ref[pl.ds(kh * 32 + QL + ql, N_DP, stride=64), :]
    return re, im


def paired(re, im):
    top = jnp.concatenate([re, im], axis=1)
    low = jnp.concatenate([im, -re], axis=1)
    return jnp.concatenate([top, low], axis=0).astype(bf16)


def mix_kernel(modes_ref, w_ref, m_ref, out_ref, m_out_ref, y_ref, sc_ref):
    m_out_ref[...] = m_ref[...]
    for n in range(N_DP):
        y_ref[n * 64 : (n + 1) * 64, :] = modes_ref[n, 64:128, :].astype(f32)
    zero = jnp.zeros((C, C), bf16)
    for kh in range(2):
        for ql in range(QL):
            lhs = paired(*load_modes(y_ref, kh, ql))
            w0, w1 = w_ref[ql, kh * 2], w_ref[ql, kh * 2 + 1]
            rhs = jnp.concatenate(
                [
                    jnp.concatenate([w0[:, :C], zero, w0[:, C:], zero], axis=1),
                    jnp.concatenate([zero, w1[:, :C], zero, w1[:, C:]], axis=1),
                ],
                axis=0,
            )
            back = dot(lhs, rhs, NT)
            sc_ref[pl.ds(kh * 32 + ql, N_DP, stride=64), :] = back[:N_DP]
            sc_ref[pl.ds(kh * 32 + QL + ql, N_DP, stride=64), :] = back[N_DP:]
    for n in range(N_DP):
        out_ref[n] = sc_ref[n * 64 : (n + 1) * 64, :].astype(bf16)


def weight_kernel(modes_ref, out_ref, x_ref, y_ref):
    for n in range(N_DP):
        x_ref[n * 64 : (n + 1) * 64, :] = modes_ref[n, 0:64, :].astype(f32)
        y_ref[n * 64 : (n + 1) * 64, :] = modes_ref[n, 64:128, :].astype(f32)
    for kh in range(2):
        for ql in range(QL):
            rhs = paired(*load_modes(y_ref, kh, ql))
            lhs = jnp.concatenate(load_modes(x_ref, kh, ql), axis=0).astype(bf16)
            grad = dot(lhs, rhs, TN)
            for kl in range(2):
                mine = grad[kl * C : (kl + 1) * C]
                re = mine[:, kl * C : (kl + 1) * C]
                im = mine[:, 128 + kl * C : 128 + (kl + 1) * C]
                out_ref[ql, kh * 2 + kl] = jnp.concatenate([re, im], axis=1).astype(bf16)


def synth_kernel(modes_ref, m_ref, out_ref, d_ref, sc_ref):
    for q in range(N_DP):
        for kh in range(2):
            d_ref[q * 32 : (q + 1) * 32, kh * 128 : (kh + 1) * 128] = modes_ref[q, kh * 32 : (kh + 1) * 32, :]
    lat = dot(m_ref[...], d_ref[...], TN)
    for part in range(2):
        for l in range(ROWS_DEV):
            at = (part * ROWS_DEV + l) * N_DOMAIN
            for kh in range(2):
                block = lat[at : at + N_DOMAIN, kh * 128 : (kh + 1) * 128]
                sc_ref[l, pl.ds(part * 2 + kh, N_DOMAIN, stride=4), :] = block
    for l in range(ROWS_DEV):
        out_ref[:, :, l * 128 : (l + 1) * 128] = sc_ref[l].reshape(N_DOMAIN, 4, 128).astype(bf16)


def grad_kernel(msg_ref, t_ref, dz_ref, pw_ref, out_hbm, sc_ref, lhs_ref, pd_ref, out_ref, sems):
    for l in range(ROWS_DEV):
        sc_ref[l] = msg_ref[:, :, l * 128 : (l + 1) * 128].astype(f32).reshape(N_DOMAIN * 4, 128)
    pd_ref[...] = jnp.zeros((LC, LC), bf16)
    for l in range(ROWS_DEV):
        blocks = [sc_ref[l, pl.ds(pk, N_DOMAIN, stride=4), :] for pk in range(4)]
        turned = jnp.concatenate(blocks, axis=0).T
        for kl in range(2):
            lhs_ref[l * C : (l + 1) * C, kl * 256 : (kl + 1) * 256] = turned[kl * C : (kl + 1) * C].astype(bf16)
        pd_ref[l * C : (l + 1) * C, l * C : (l + 1) * C] = pw_ref[...]
    copies = []
    for lo, hi in zip(EDGES[:-1], EDGES[1:]):
        cols = slice(lo, hi)
        even = dot(lhs_ref[:, :256], t_ref[:256, cols], NN)
        odd = dot(lhs_ref[:, 256:], t_ref[256:, cols], NN)
        for h, spec in enumerate((even + odd, even - odd)):
            cols = slice(h * HALF + lo, h * HALF + hi)
            out_ref[:, cols] = (spec + dot(pd_ref[...], dz_ref[:, cols], NN)).astype(bf16)
            copies.append(pltpu.make_async_copy(out_ref.at[:, cols], out_hbm.at[:, cols], sems.at[len(copies)]))
            copies[-1].start()
    for copy in copies:
        copy.wait()


WHOLE = pl.BlockSpec(memory_space=pltpu.VMEM)
FAR = pl.BlockSpec(memory_space=pltpu.HBM)


def call(kernel, outs, scratch, flops, *args, specs=None, out_specs=None, vmem=40):
    nbytes = sum(a.size * a.dtype.itemsize for a in args)
    return pl.pallas_call(
        kernel,
        out_shape=outs,
        in_specs=specs or [WHOLE] * len(args),
        out_specs=jax.tree.map(lambda _: WHOLE, outs) if out_specs is None else out_specs,
        scratch_shapes=scratch,
        cost_estimate=pl.CostEstimate(flops=flops, bytes_accessed=nbytes, transcendentals=0),
        compiler_params=pltpu.CompilerParams(vmem_limit_bytes=vmem * 1024 * 1024),
    )(*args)


def slots_call(inputs, preact, table, readout, observed, cell_index, drift_steps, counts, weight, lat):
    small = [pltpu.VMEM((1, SLOTS), jnp.int32), pltpu.VMEM((1, SLOTS), jnp.int32)]
    return call(
        slots_kernel,
        (
            jax.ShapeDtypeStruct((N_DOMAIN, 8, 384), bf16),
            jax.ShapeDtypeStruct((C, SLOTS), f32),
            jax.ShapeDtypeStruct(weight.shape, bf16),
            jax.ShapeDtypeStruct(lat.shape, bf16),
        ),
        [
            pltpu.VMEM((HALF, SLOTS), bf16),
            pltpu.VMEM((512, SLOTS), bf16),
            pltpu.VMEM((ROWS_DEV, 512, 128), f32),
            pltpu.VMEM((LC, NX), bf16),
            pltpu.VMEM((2 * LC, HALF), bf16),
            pltpu.VMEM((512, HALF), bf16),
            pltpu.VMEM((STEPS, 2, C), f32),
            pltpu.VMEM((2, SLOTS), f32),
            *small,
            pltpu.SemaphoreType.DMA((10,)),
        ],
        2 * LC * NX * 512 * 4,
        *[
            pltpu.with_memory_space_constraint(array, pltpu.HBM)
            for array in (
                inputs.reshape(LC, NX),
                preact.reshape(LC, NX),
                table,
                readout,
                observed.reshape(2, SLOTS),
                cell_index,
                drift_steps,
                weight,
                lat,
            )
        ],
        counts,
        specs=[FAR] * 9 + [pl.BlockSpec(memory_space=pltpu.SMEM)],
    )


def grad_call(msg, table, dz, point_weight):
    return call(
        grad_kernel,
        jax.ShapeDtypeStruct((LC, NX), bf16),
        [
            pltpu.VMEM((ROWS_DEV, 256, 128), f32),
            pltpu.VMEM((LC, 512), bf16),
            pltpu.VMEM((LC, LC), bf16),
            pltpu.VMEM((LC, NX), bf16),
            pltpu.SemaphoreType.DMA((2 * len(EDGES),)),
        ],
        2 * LC * NX * 448,
        msg,
        table,
        dz,
        point_weight,
        out_specs=FAR,
    )


def local(inputs, preact, spectral_weight, point_weight, readout, observed, cell_index, drift_steps, counts):
    table = jnp.asarray(lon_table())
    lat = jnp.asarray(lat_table())
    msg, dslot, weight, lat = slots_call(
        inputs, preact, table, readout, observed, cell_index, drift_steps, counts, spectral_weight, lat
    )
    msg = lax.all_to_all(msg, "domain", 0, 0, tiled=True)
    modes = call(
        lat_kernel,
        jax.ShapeDtypeStruct((N_DP, 128, 128), bf16),
        [pltpu.VMEM((ROWS_DEV, 512, 128), f32), pltpu.VMEM((384, 512), bf16)],
        2 * 256 * 384 * 512,
        msg,
        lat,
    )
    modes = lax.all_to_all(modes, "dp", 0, 0, tiled=True)
    dmodes, lat = call(
        mix_kernel,
        (jax.ShapeDtypeStruct((N_DP, 64, 128), bf16), jax.ShapeDtypeStruct(lat.shape, bf16)),
        [pltpu.VMEM((512, 128), f32), pltpu.VMEM((512, 128), f32)],
        2 * 32 * 128 * 128 * 256,
        modes,
        weight,
        lat,
    )
    dmodes = lax.all_to_all(dmodes, "dp", 0, 0, tiled=True)
    weight_grad = call(
        weight_kernel,
        jax.ShapeDtypeStruct((QL, 4, C, 2 * C), bf16),
        [pltpu.VMEM((512, 128), f32), pltpu.VMEM((512, 128), f32)],
        2 * 32 * 128 * 128 * 256,
        modes,
    )
    dz = call(
        scatter_kernel,
        jax.ShapeDtypeStruct((LC, NX), bf16),
        [pltpu.VMEM((NX, SLOTS), bf16)],
        2 * LC * NX * 512 * 2,
        dslot,
        cell_index,
    )
    msg = call(
        synth_kernel,
        jax.ShapeDtypeStruct((N_DOMAIN, 4, 384), bf16),
        [
            pltpu.VMEM((256, 256), bf16),
            pltpu.VMEM((ROWS_DEV, 256, 128), f32),
        ],
        2 * 256 * 384 * 256,
        dmodes,
        lat,
    )
    msg = lax.all_to_all(msg, "domain", 0, 0, tiled=True)
    input_grad = grad_call(msg, table, dz, point_weight)
    return (input_grad.reshape(1, ROWS_DEV, C, NX), weight_grad)


def solution(mesh):
    placed = (
        P("dp", "domain", None, None),
        P("dp", "domain", None, None),
        P("dp", "domain", None, None),
        P(),
        P(),
        P("dp", None, "domain"),
        P("dp", "domain"),
        P("dp", "domain"),
        P("dp", "domain"),
    )
    return jax.shard_map(
        local,
        mesh=mesh,
        in_specs=placed,
        out_specs=(P("dp", "domain", None, None), P("dp", "domain", None, None)),
        check_vma=False,
    )
```

```python
import numpy as np
import ml_dtypes
import jax
import jax.numpy as jnp
from jax import lax
from jax.experimental import pallas as pl
from jax.experimental.pallas import tpu as pltpu
from jax.sharding import PartitionSpec as P

NX = 2304
NY = 2160
KX = 256
KY = 128
STEPS = 48
SLOTS = 512
C = 64
ROWS_DEV = 3
N_DOMAIN = 64
N_DP = 8
ROWS = ROWS_DEV * N_DOMAIN
QL = KY // N_DP
LC = ROWS_DEV * C
HALF = NX // 2
EDGES = (0, 640, 1152)

two_pi = 6.283185307179586
loss_scale = 8.0
gelu_a = 0.7978845608
gelu_b = 0.044715

f32 = jnp.float32
bf16 = jnp.bfloat16


def lon_table():
    kl, part, kh, block = np.meshgrid(np.arange(2), np.arange(2), np.arange(2), np.arange(N_DOMAIN), indexing="ij")
    wavenum = (4 * block + 2 * kh + kl).reshape(-1, 1).astype(np.int64)
    part = part.reshape(-1, 1)
    phase = (wavenum * np.arange(HALF)[None, :] % NX) * (two_pi / NX)
    return np.where(part == 0, np.cos(phase), -np.sin(phase)).astype(ml_dtypes.bfloat16)


def lat_table():
    block, part, ql = np.meshgrid(np.arange(N_DP), np.arange(2), np.arange(QL), indexing="ij")
    part2, l, slab = np.meshgrid(np.arange(2), np.arange(ROWS_DEV), np.arange(N_DOMAIN), indexing="ij")
    index_q = (block * QL + ql).reshape(-1, 1)
    wavenum = np.where(index_q < KY // 2, index_q, NY - KY + index_q).astype(np.int64)
    rows_y = (slab * ROWS_DEV + l).reshape(1, -1) * (NY // ROWS)
    phase = (wavenum * rows_y % NY) * (two_pi / NY)
    part, part2 = part.reshape(-1, 1), part2.reshape(1, -1)
    sine = np.where(part < part2, np.sin(phase), -np.sin(phase))
    return np.where(part == part2, np.cos(phase), sine).astype(ml_dtypes.bfloat16)


def dot(a, b, contract, precision=None):
    return lax.dot_general(a, b, ((contract[0], contract[1]), ((), ())), precision=precision, preferred_element_type=f32)


NN = ((1,), (0,))
NT = ((1,), (1,))
TN = ((0,), (0,))


def where_slots(cell_ref):
    cell = cell_ref[...]
    row = (cell >= NX).astype(jnp.int32) + (cell >= 2 * NX).astype(jnp.int32)
    return row, cell - row * NX


def hot_slots(col, oh_ref):
    step = 128
    for i in range(oh_ref.shape[0] // step):
        here = lax.broadcasted_iota(jnp.int32, (step, SLOTS), 0) + i * step
        oh_ref[i * step : (i + 1) * step, :] = (here == col).astype(f32).astype(bf16)


def turn(steps):
    steps = steps - NX * jnp.floor(steps * (1.0 / NX) + 0.5)
    quarter = jnp.floor(steps * (4.0 / NX) + 0.5)
    a = (steps - (NX // 4) * quarter) * (two_pi / NX)
    b = a * a
    cosine = 1.0 + b * (-1 / 2 + b * (1 / 24 + b * (-1 / 720 + b * (1 / 40320))))
    sine = a * (1.0 + b * (-1 / 6 + b * (1 / 120 + b * (-1 / 5040 + b * (1 / 362880)))))
    odd = jnp.abs(quarter) == 1.0
    cosine, sine = jnp.where(odd, sine, cosine), jnp.where(odd, cosine, sine)
    cosine = jnp.where((quarter == 1.0) | (jnp.abs(quarter) == 2.0), -cosine, cosine)
    return cosine, jnp.where((quarter < 0.0) | (quarter == 2.0), -sine, sine)


def slot_waves(col, out_ref):
    x = col.astype(f32)
    block = lax.broadcasted_iota(jnp.int32, (N_DOMAIN, SLOTS), 0).astype(f32)
    cos4, sin4 = turn(4.0 * block * x)
    for kl in range(2):
        for kh in range(2):
            cosj, sinj = turn((2.0 * kh + kl) * x)
            at = kl * 256 + kh * 64
            out_ref[at : at + 64, :] = (cos4 * cosj - sin4 * sinj).astype(bf16)
            out_ref[at + 128 : at + 192, :] = (-sin4 * cosj - cos4 * sinj).astype(bf16)


def spread_slots(row, dslot):
    hi = dslot.astype(bf16).astype(f32)
    lo = dslot - hi
    zero = jnp.zeros((C, SLOTS), f32)
    return [
        jnp.concatenate([jnp.where(row == l, part, zero).astype(bf16) for l in range(ROWS_DEV)], axis=0)
        for part in (hi, lo)
    ]


def slots_kernel(
    x_hbm, p_hbm, t_hbm, ro_hbm, obs_hbm, cell_hbm, step_hbm, w_hbm, m_hbm, cnt_ref, msg_ref, dslot_ref, w_ref, m_ref, oh_ref, wave_ref, sc_ref, x_ref, p_ref, t_ref, ro_ref, obs_ref, cell_ref, step_ref, sems,
):
    moves = (
        (cell_hbm, cell_ref),
        (step_hbm, step_ref),
        (obs_hbm, obs_ref),
        (ro_hbm, ro_ref),
        (p_hbm.at[:, :HALF], p_ref.at[:LC]),
        (p_hbm.at[:, HALF:], p_ref.at[LC:]),
        (t_hbm, t_ref),
        (x_hbm, x_ref),
        (m_hbm, m_ref),
        (w_hbm, w_ref),
    )
    copies = [pltpu.make_async_copy(src, dst, sems.at[i]) for i, (src, dst) in enumerate(moves)]
    for copy in copies:
        copy.start()
    copies[0].wait()
    row, col = where_slots(cell_ref)
    east = (col >= HALF).astype(jnp.int32)
    hot_slots(col - east * HALF, oh_ref)
    slot_waves(col, wave_ref)
    place = east * ROWS_DEV + row
    for copy in copies[1:4]:
        copy.wait()
    step_hot = (lax.broadcasted_iota(jnp.int32, (STEPS, SLOTS), 0) == step_ref[...]).astype(f32).astype(bf16)
    step_hot = jnp.concatenate([step_hot] * 3, axis=0)
    chosen = []
    for j in range(2):
        full = ro_ref[:, j, :]
        top = full.astype(bf16)
        mid = (full - top.astype(f32)).astype(bf16)
        low = (full - top.astype(f32) - mid.astype(f32)).astype(bf16)
        chosen.append(dot(jnp.concatenate([top, mid, low], axis=0), step_hot, TN))
    for copy in copies[4:6]:
        copy.wait()
    zall = dot(p_ref[...], oh_ref[...], NN)
    z = jnp.zeros((C, SLOTS), f32)
    for i in range(2 * ROWS_DEV):
        z = z + jnp.where(place == i, zall[i * C : (i + 1) * C], 0.0)
    th = jnp.tanh(gelu_a * (z + gelu_b * (z * z * z)))
    act = 0.5 * z * (1.0 + th)
    slope = 0.5 * (1.0 + th) + 0.5 * z * (1.0 - th * th) * (gelu_a * (1.0 + 3.0 * gelu_b * (z * z)))
    live = (lax.broadcasted_iota(jnp.int32, (1, SLOTS), 1) < cnt_ref[0, 0]).astype(f32)
    back = jnp.zeros((C, SLOTS), f32)
    for j in range(2):
        cj = chosen[j]
        velocity = jnp.sum(cj * act, axis=0, keepdims=True)
        back = back + cj * (loss_scale * live * (velocity - obs_ref[j : j + 1, :]))
    dslot = slope * back
    dslot_ref[...] = dslot

    def place_spectra(xz, even, odd):
        for l in range(ROWS_DEV):
            for pk in range(4):
                block = jnp.concatenate(
                    [spec[pk * 64 : (pk + 1) * 64, l * C : (l + 1) * C] for spec in (even, odd)], axis=1
                )
                sc_ref[l, pl.ds(xz * 4 + pk, N_DOMAIN, stride=8), :] = block

    copies[6].wait()
    copies[7].wait()
    near, far = x_ref[:, :HALF].astype(f32), x_ref[:, HALF:].astype(f32)
    place_spectra(
        0, dot(t_ref[:256], (near + far).astype(bf16), NT), dot(t_ref[256:], (near - far).astype(bf16), NT)
    )
    hi, lo = spread_slots(row, dslot)
    both = jnp.concatenate([hi, lo], axis=0)
    parts = [dot(waves, both, NT) for waves in (wave_ref[:256], wave_ref[256:])]
    place_spectra(1, *[spec[:, :LC] + spec[:, LC:] for spec in parts])
    for l in range(ROWS_DEV):
        msg_ref[:, :, l * 128 : (l + 1) * 128] = sc_ref[l].reshape(N_DOMAIN, 8, 128).astype(bf16)
    copies[8].wait()
    copies[9].wait()


def scatter_kernel(dslot_ref, cell_ref, dz_ref, oh_ref):
    row, col = where_slots(cell_ref)
    hot_slots(col, oh_ref)
    both = jnp.concatenate(spread_slots(row, dslot_ref[...]), axis=0)
    step = 768
    for i in range(NX // step):
        grid = dot(both, oh_ref[i * step : (i + 1) * step, :], NT)
        dz_ref[:, i * step : (i + 1) * step] = (grid[:LC] + grid[LC:]).astype(bf16)


def lat_kernel(msg_ref, m_ref, out_ref, sc_ref, rhs_ref):
    for l in range(ROWS_DEV):
        sc_ref[l] = msg_ref[:, :, l * 128 : (l + 1) * 128].astype(f32).reshape(N_DOMAIN * 8, 128)
    for xz in range(2):
        for part in range(2):
            for kh in range(2):
                for l in range(ROWS_DEV):
                    block = sc_ref[l, pl.ds(xz * 4 + part * 2 + kh, N_DOMAIN, stride=8), :]
                    at, lane = (part * ROWS_DEV + l) * N_DOMAIN, (xz * 2 + kh) * 128
                    rhs_ref[at : at + N_DOMAIN, lane : lane + 128] = block.astype(bf16)
    lead = (lax.axis_index("domain") == 0) & (lax.broadcasted_iota(jnp.int32, (1, 256), 1) < C)
    scale = jnp.where(lead, 1.0 / (NX * ROWS), 2.0 / (NX * ROWS))
    modes = dot(m_ref[...], rhs_ref[...], NN)
    for xz in range(2):
        for kh in range(2):
            b = xz * 2 + kh
            part = modes[:, b * 128 : (b + 1) * 128]
            if xz == 1:
                part = part * scale[:, kh * 128 : (kh + 1) * 128]
            part = part.astype(bf16)
            for d in range(N_DP):
                out_ref[d, b * 32 : (b + 1) * 32, :] = part[d * 32 : (d + 1) * 32]


def load_modes(ref, kh, ql):
    re = ref[pl.ds(kh * 32 + ql, N_DP, stride=64), :]
    im = ref[pl.ds(kh * 32 + QL + ql, N_DP, stride=64), :]
    return re, im


def paired(re, im):
    top = jnp.concatenate([re, im], axis=1)
    low = jnp.concatenate([im, -re], axis=1)
    return jnp.concatenate([top, low], axis=0).astype(bf16)


def mix_kernel(modes_ref, w_ref, m_ref, out_ref, m_out_ref, y_ref, sc_ref):
    m_out_ref[...] = m_ref[...]
    for n in range(N_DP):
        y_ref[n * 64 : (n + 1) * 64, :] = modes_ref[n, 64:128, :].astype(f32)
    zero = jnp.zeros((C, C), bf16)
    for kh in range(2):
        for ql in range(QL):
            lhs = paired(*load_modes(y_ref, kh, ql))
            w0, w1 = w_ref[ql, kh * 2], w_ref[ql, kh * 2 + 1]
            rhs = jnp.concatenate(
                [
                    jnp.concatenate([w0[:, :C], zero, w0[:, C:], zero], axis=1),
                    jnp.concatenate([zero, w1[:, :C], zero, w1[:, C:]], axis=1),
                ],
                axis=0,
            )
            back = dot(lhs, rhs, NT)
            sc_ref[pl.ds(kh * 32 + ql, N_DP, stride=64), :] = back[:N_DP]
            sc_ref[pl.ds(kh * 32 + QL + ql, N_DP, stride=64), :] = back[N_DP:]
    for n in range(N_DP):
        out_ref[n] = sc_ref[n * 64 : (n + 1) * 64, :].astype(bf16)


def weight_kernel(modes_ref, out_ref, x_ref, y_ref):
    for n in range(N_DP):
        x_ref[n * 64 : (n + 1) * 64, :] = modes_ref[n, 0:64, :].astype(f32)
        y_ref[n * 64 : (n + 1) * 64, :] = modes_ref[n, 64:128, :].astype(f32)
    for kh in range(2):
        for ql in range(QL):
            rhs = paired(*load_modes(y_ref, kh, ql))
            lhs = jnp.concatenate(load_modes(x_ref, kh, ql), axis=0).astype(bf16)
            grad = dot(lhs, rhs, TN)
            for kl in range(2):
                mine = grad[kl * C : (kl + 1) * C]
                re = mine[:, kl * C : (kl + 1) * C]
                im = mine[:, 128 + kl * C : 128 + (kl + 1) * C]
                out_ref[ql, kh * 2 + kl] = jnp.concatenate([re, im], axis=1).astype(bf16)


def synth_kernel(modes_ref, m_ref, out_hbm, d_ref, sc_ref, out_ref, sems):
    for q in range(N_DP):
        for kh in range(2):
            d_ref[q * 32 : (q + 1) * 32, kh * 128 : (kh + 1) * 128] = modes_ref[q, kh * 32 : (kh + 1) * 32, :]
    lat = dot(m_ref[...], d_ref[...], TN)
    for part in range(2):
        for l in range(ROWS_DEV):
            at = (part * ROWS_DEV + l) * N_DOMAIN
            for kh in range(2):
                block = lat[at : at + N_DOMAIN, kh * 128 : (kh + 1) * 128]
                sc_ref[l, pl.ds(part * 2 + kh, N_DOMAIN, stride=4), :] = block
    copies = []
    for l in range(ROWS_DEV):
        lanes = slice(l * 128, (l + 1) * 128)
        out_ref[:, :, lanes] = sc_ref[l].reshape(N_DOMAIN, 4, 128).astype(bf16)
        copies.append(pltpu.make_async_copy(out_ref.at[:, :, lanes], out_hbm.at[:, :, lanes], sems.at[l]))
        copies[-1].start()
    for copy in copies:
        copy.wait()


def grad_kernel(msg_ref, t_ref, dz_ref, pw_ref, out_hbm, sc_ref, lhs_ref, pd_ref, out_ref, sems):
    for l in range(ROWS_DEV):
        sc_ref[l] = msg_ref[:, :, l * 128 : (l + 1) * 128].astype(f32).reshape(N_DOMAIN * 4, 128)
    pd_ref[...] = jnp.zeros((LC, LC), bf16)
    for l in range(ROWS_DEV):
        blocks = [sc_ref[l, pl.ds(pk, N_DOMAIN, stride=4), :] for pk in range(4)]
        turned = jnp.concatenate(blocks, axis=0).T
        for kl in range(2):
            lhs_ref[l * C : (l + 1) * C, kl * 256 : (kl + 1) * 256] = turned[kl * C : (kl + 1) * C].astype(bf16)
        pd_ref[l * C : (l + 1) * C, l * C : (l + 1) * C] = pw_ref[...]
    copies = []
    for lo, hi in zip(EDGES[:-1], EDGES[1:]):
        cols = slice(lo, hi)
        even = dot(lhs_ref[:, :256], t_ref[:256, cols], NN)
        odd = dot(lhs_ref[:, 256:], t_ref[256:, cols], NN)
        for h, spec in enumerate((even + odd, even - odd)):
            cols = slice(h * HALF + lo, h * HALF + hi)
            out_ref[:, cols] = (spec + dot(pd_ref[...], dz_ref[:, cols], NN)).astype(bf16)
            copies.append(pltpu.make_async_copy(out_ref.at[:, cols], out_hbm.at[:, cols], sems.at[len(copies)]))
            copies[-1].start()
    for copy in copies:
        copy.wait()


WHOLE = pl.BlockSpec(memory_space=pltpu.VMEM)
FAR = pl.BlockSpec(memory_space=pltpu.HBM)


def call(kernel, outs, scratch, flops, *args, specs=None, out_specs=None, vmem=40):
    nbytes = sum(a.size * a.dtype.itemsize for a in args)
    return pl.pallas_call(
        kernel,
        out_shape=outs,
        in_specs=specs or [WHOLE] * len(args),
        out_specs=jax.tree.map(lambda _: WHOLE, outs) if out_specs is None else out_specs,
        scratch_shapes=scratch,
        cost_estimate=pl.CostEstimate(flops=flops, bytes_accessed=nbytes, transcendentals=0),
        compiler_params=pltpu.CompilerParams(vmem_limit_bytes=vmem * 1024 * 1024),
    )(*args)


def slots_call(inputs, preact, table, readout, observed, cell_index, drift_steps, counts, weight, lat):
    small = [pltpu.VMEM((1, SLOTS), jnp.int32), pltpu.VMEM((1, SLOTS), jnp.int32)]
    return call(
        slots_kernel,
        (
            jax.ShapeDtypeStruct((N_DOMAIN, 8, 384), bf16),
            jax.ShapeDtypeStruct((C, SLOTS), f32),
            jax.ShapeDtypeStruct(weight.shape, bf16),
            jax.ShapeDtypeStruct(lat.shape, bf16),
        ),
        [
            pltpu.VMEM((HALF, SLOTS), bf16),
            pltpu.VMEM((512, SLOTS), bf16),
            pltpu.VMEM((ROWS_DEV, 512, 128), f32),
            pltpu.VMEM((LC, NX), bf16),
            pltpu.VMEM((2 * LC, HALF), bf16),
            pltpu.VMEM((512, HALF), bf16),
            pltpu.VMEM((STEPS, 2, C), f32),
            pltpu.VMEM((2, SLOTS), f32),
            *small,
            pltpu.SemaphoreType.DMA((10,)),
        ],
        2 * LC * NX * 512 * 4,
        *[
            pltpu.with_memory_space_constraint(array, pltpu.HBM)
            for array in (
                inputs.reshape(LC, NX),
                preact.reshape(LC, NX),
                table,
                readout,
                observed.reshape(2, SLOTS),
                cell_index,
                drift_steps,
                weight,
                lat,
            )
        ],
        counts,
        specs=[FAR] * 9 + [pl.BlockSpec(memory_space=pltpu.SMEM)],
    )


def grad_call(msg, table, dz, point_weight):
    return call(
        grad_kernel,
        jax.ShapeDtypeStruct((LC, NX), bf16),
        [
            pltpu.VMEM((ROWS_DEV, 256, 128), f32),
            pltpu.VMEM((LC, 512), bf16),
            pltpu.VMEM((LC, LC), bf16),
            pltpu.VMEM((LC, NX), bf16),
            pltpu.SemaphoreType.DMA((2 * len(EDGES),)),
        ],
        2 * LC * NX * 448,
        msg,
        table,
        dz,
        point_weight,
        out_specs=FAR,
    )


def local(inputs, preact, spectral_weight, point_weight, readout, observed, cell_index, drift_steps, counts):
    table = jnp.asarray(lon_table())
    lat = jnp.asarray(lat_table())
    msg, dslot, weight, lat = slots_call(
        inputs, preact, table, readout, observed, cell_index, drift_steps, counts, spectral_weight, lat
    )
    msg = lax.all_to_all(msg, "domain", 0, 0, tiled=True)
    modes = call(
        lat_kernel,
        jax.ShapeDtypeStruct((N_DP, 128, 128), bf16),
        [pltpu.VMEM((ROWS_DEV, 512, 128), f32), pltpu.VMEM((384, 512), bf16)],
        2 * 256 * 384 * 512,
        msg,
        lat,
    )
    modes = lax.all_to_all(modes, "dp", 0, 0, tiled=True)
    dmodes, lat = call(
        mix_kernel,
        (jax.ShapeDtypeStruct((N_DP, 64, 128), bf16), jax.ShapeDtypeStruct(lat.shape, bf16)),
        [pltpu.VMEM((512, 128), f32), pltpu.VMEM((512, 128), f32)],
        2 * 32 * 128 * 128 * 256,
        modes,
        weight,
        lat,
    )
    dmodes = lax.all_to_all(dmodes, "dp", 0, 0, tiled=True)
    weight_grad = call(
        weight_kernel,
        jax.ShapeDtypeStruct((QL, 4, C, 2 * C), bf16),
        [pltpu.VMEM((512, 128), f32), pltpu.VMEM((512, 128), f32)],
        2 * 32 * 128 * 128 * 256,
        modes,
    )
    dz = call(
        scatter_kernel,
        jax.ShapeDtypeStruct((LC, NX), bf16),
        [pltpu.VMEM((NX, SLOTS), bf16)],
        2 * LC * NX * 512 * 2,
        dslot,
        cell_index,
    )
    msg = call(
        synth_kernel,
        pltpu.HBM((N_DOMAIN, 4, 384), bf16),
        [
            pltpu.VMEM((256, 256), bf16),
            pltpu.VMEM((ROWS_DEV, 256, 128), f32),
            pltpu.VMEM((N_DOMAIN, 4, 384), bf16),
            pltpu.SemaphoreType.DMA((ROWS_DEV,)),
        ],
        2 * 256 * 384 * 256,
        dmodes,
        lat,
        out_specs=FAR,
    )
    msg = lax.all_to_all(msg, "domain", 0, 0, tiled=True)
    input_grad = grad_call(msg, table, dz, point_weight)
    return (input_grad.reshape(1, ROWS_DEV, C, NX), weight_grad)


def solution(mesh):
    placed = (
        P("dp", "domain", None, None),
        P("dp", "domain", None, None),
        P("dp", "domain", None, None),
        P(),
        P(),
        P("dp", None, "domain"),
        P("dp", "domain"),
        P("dp", "domain"),
        P("dp", "domain"),
    )
    return jax.shard_map(
        local,
        mesh=mesh,
        in_specs=placed,
        out_specs=(P("dp", "domain", None, None), P("dp", "domain", None, None)),
        check_vma=False,
    )
```
